256 devices in a mesh: img: 8 (over x, y_hi), txt: 32 (over y_lo, z, core).
Axes of the slice: x: 4, y: 4 (y_hi: 2, y_lo: 2; y = y_hi * 2 + y_lo), z: 8, core: 2. Of those that a mesh axis runs over, the one named last changes fastest.
Arguments:
- image: bfloat16 [16384, 1280], P(('img', 'txt')), may hold values from -8 to 8
- text: bfloat16 [16384, 1280], P(('txt', 'img')), may hold values from -8 to 8
Outputs:
- image_grad: bfloat16 [16384, 1280], P(('img', 'txt'))
- text_grad: bfloat16 [16384, 1280], P(('txt', 'img'))
- loss: float32 [], replicated
The draws below stay inside these ranges and needn't reach their ends.
All inputs are finite; a program needn't handle non-finite values.
Results may differ from the reference program's by a relative error of at most 0.0034.
Values may be sent and summed in bfloat16 or wider, within the bound.
No kernel may reach another device: no remote copies, remote signals or barrier semaphores. Data moves between devices by JAX's collectives and lax.ppermute only.
A program may use at most 64 MiB of HBM per device.

```python
import math
import jax
import jax.numpy as jnp
from jax import lax

EMBED = 1280
PAIRS = 16384
IMG_BLOCK = 2048
N_IMG = 8


def draw_image(key, part):
    key = jax.random.fold_in(key, 1)
    values = jax.random.normal(key, (PAIRS, EMBED), jnp.float32)
    return jnp.clip(values, -8.0, 8.0).astype(jnp.bfloat16)


def draw_text(key, part):
    key = jax.random.fold_in(key, 2)
    values = jax.random.normal(key, (PAIRS, EMBED), jnp.float32)
    return jnp.clip(values, -8.0, 8.0).astype(jnp.bfloat16)


def setup_inputs(seed: int = 0) -> dict:
    keys = jax.random.split(jax.random.key(seed), 3)
    return {
        "image": draw_image(jax.random.fold_in(keys[2], 71), 0),
        "text": draw_text(jax.random.fold_in(keys[2], 71), 0),
    }


def reference(image, text):
    logit_scale = 4.0 / math.sqrt(EMBED)
    img_blocks = image.reshape(N_IMG, IMG_BLOCK, EMBED)
    block_ids = jnp.arange(N_IMG, dtype=jnp.int32)

    def scores_of(block):
        return logit_scale * jnp.dot(block, text.T, preferred_element_type=jnp.float32)

    def first_pass(carry, inputs):
        col_top, col_sum = carry
        block, index = inputs
        scores = scores_of(block)
        row_top = lax.optimization_barrier(jnp.max(scores, axis=1, keepdims=True))
        row_lse = row_top[:, 0] + jnp.log(lax.optimization_barrier(jnp.sum(jnp.exp(scores - row_top), axis=1)))
        new_top = jnp.maximum(col_top, lax.optimization_barrier(jnp.max(scores, axis=0)))
        new_sum = col_sum * jnp.exp(col_top - new_top) + lax.optimization_barrier(jnp.sum(jnp.exp(scores - new_top[None, :]), axis=0))
        square = lax.dynamic_slice_in_dim(scores, (index * IMG_BLOCK).astype(jnp.int32), IMG_BLOCK, 1)
        return ((new_top, new_sum), (row_lse, jnp.trace(square)))
    start = (jnp.full((PAIRS,), -1e+30, jnp.float32), jnp.zeros((PAIRS,), jnp.float32))
    (col_top, col_sum), (row_lse, diag_sums) = lax.scan(first_pass, start, (img_blocks, block_ids))
    col_lse = col_top + jnp.log(col_sum)
    loss = (0.5 * (jnp.sum(row_lse) + jnp.sum(col_lse)) - jnp.sum(diag_sums)) / PAIRS

    def second_pass(text_acc, inputs):
        block, index, block_lse = inputs
        scores = scores_of(block)
        rows = index * IMG_BLOCK + jnp.arange(IMG_BLOCK, dtype=jnp.int32)[:, None]
        cols = jnp.arange(PAIRS, dtype=jnp.int32)[None, :]
        diagonal = (rows == cols).astype(jnp.float32)
        weights = ((jnp.exp(scores - block_lse[:, None]) + jnp.exp(scores - col_lse[None, :])) * 0.5 - diagonal).astype(jnp.bfloat16)
        img_grad = jnp.dot(weights, text, preferred_element_type=jnp.float32).astype(jnp.bfloat16)
        term = jnp.dot(weights.T, block, preferred_element_type=jnp.float32)
        return (text_acc + term, img_grad)
    text_acc, img_grads = lax.scan(second_pass, jnp.zeros((PAIRS, EMBED), jnp.float32), (img_blocks, block_ids, row_lse))
    image_grad = img_grads.reshape(PAIRS, EMBED)
    return (image_grad, text_acc.astype(jnp.bfloat16), loss)
```

```python
import functools
import math

import jax
import jax.numpy as jnp
from jax import lax
from jax.experimental import pallas as pl
from jax.experimental.pallas import tpu as pltpu
from jax.sharding import PartitionSpec as P

NX, NY, NZ, NC = 4, 4, 8, 2
AXES = ("img", "txt")
SHARD = 64
HALF = SHARD // 2
ROWS = NZ * NC * SHARD
COLS = NX * NY * SHARD
CORE_ROWS = NZ * SHARD
BF16, F32 = jnp.bfloat16, jnp.float32
VMEM_LIMIT = 48 * 1024 * 1024


def device_id(x, y, z, c):
    return (((x % NX) * NY + y % NY) * NZ + z % NZ) * NC + c % NC


def coordinates():
    return [(x, y, z, c) for x in range(NX) for y in range(NY) for z in range(NZ) for c in range(NC)]


def shift(value, x=0, y=0, z=0, c=0):
    pairs = [
        (device_id(*at), device_id(at[0] + x, at[1] + y, at[2] + z, at[3] + c)) for at in coordinates()
    ]
    return lax.ppermute(value, AXES, pairs)


def swap(value, axis, bit):
    pairs = []
    for at in coordinates():
        to = list(at)
        to[axis] ^= bit
        pairs.append((device_id(*at), device_id(*to)))
    return lax.ppermute(value, AXES, pairs)


def ring_step(value):
    pairs = [(device_id(x, y, z, c), device_id(x, y, z + 1 - 2 * c, c)) for x, y, z, c in coordinates()]
    return lax.ppermute(value, AXES, pairs)


def merge(first, second):
    top = jnp.maximum(first, second)
    return top + jnp.log(jnp.exp(first - top) + jnp.exp(second - top))


def call(kernel, out_shape, n_in, in_vmem, scratch, flops, transcendentals, moved, *args):
    any_space = pl.BlockSpec(memory_space=pl.ANY)
    vmem = pl.BlockSpec(memory_space=pltpu.VMEM)
    return pl.pallas_call(
        kernel,
        out_shape=[shape for shape, _ in out_shape],
        in_specs=[pl.BlockSpec(memory_space=pltpu.SMEM)]
        + [vmem if i in in_vmem else any_space for i in range(n_in)],
        out_specs=[vmem if in_v else any_space for _, in_v in out_shape],
        scratch_shapes=scratch,
        cost_estimate=pl.CostEstimate(flops=flops, transcendentals=transcendentals, bytes_accessed=moved),
        compiler_params=pltpu.CompilerParams(vmem_limit_bytes=VMEM_LIMIT),
    )(*args)


def diagonal_blocks(x, c):
    for xx in range(NX):
        for yh in range(2):
            yield yh * CORE_ROWS + (c * 4 + xx) * SHARD, (xx * NY + yh * 2) * SHARD


def on_diagonal(x):
    rows = lax.broadcasted_iota(jnp.int32, (SHARD, 128), 0)
    lanes = lax.broadcasted_iota(jnp.int32, (SHARD, 128), 1)
    return lanes == rows + (x // 2) * SHARD


def has_diagonal(x, y, z):
    return z == (x % 2) * 4 + y


def scores_kernel(scale, at, *refs):
    image_in, text_in = refs[:9], refs[9:17]
    scores_out, img_out, txt_out, row_out, col_out, diag_out = refs[17:23]
    img, txt, scores, row_col, sem_in, sem_out = refs[23:]
    x, y, z, c = at[0], at[1], at[2], at[3]
    sign = 1 - 2 * c
    copies = []

    def load(src, dst):
        copy = pltpu.make_async_copy(src, dst, sem_in.at[len(copies)])
        copy.start()
        copies.append(copy)

    def col_block(xx, yy):
        return (lax.rem(xx + NX, NX) * NY + lax.rem(yy + NY, NY)) * SHARD

    for i, d in enumerate((0, 1, -1, 2)):
        for j, e in enumerate((0, 1, -1, 2)):
            load(
                text_in[i].at[pl.ds(j * HALF, HALF)],
                txt.at[pl.ds(pl.multiple_of(col_block(x - d, y - e), SHARD), HALF)],
            )
            load(
                text_in[4 + i].at[pl.ds(j * HALF, HALF)],
                txt.at[pl.ds(pl.multiple_of(col_block(x - e, y - d) + HALF, HALF), HALF)],
            )
    n_text = len(copies)
    for k, ref in enumerate(image_in[:7]):
        step = (0, -1, -2, -3, 1, 2, 3)[k]
        where = lax.rem(z + sign * step + NZ, NZ) * SHARD
        for cc in range(NC):
            load(
                ref.at[pl.ds(cc * SHARD, SHARD)],
                img.at[pl.ds(pl.multiple_of(cc * CORE_ROWS + where, SHARD), SHARD)],
            )
    far = lax.rem(z + 4, NZ) * SHARD
    load(image_in[7], img.at[pl.ds(pl.multiple_of(c * CORE_ROWS + far, SHARD), SHARD)])
    load(image_in[8], img.at[pl.ds(pl.multiple_of((1 - c) * CORE_ROWS + far, SHARD), SHARD)])
    for copy in copies:
        copy.wait()
    out_img = pltpu.make_async_copy(img, img_out, sem_out.at[0])
    out_img.start()
    out_txt = pltpu.make_async_copy(txt, txt_out, sem_out.at[1])
    out_txt.start()

    chunk = 256
    outs = []
    col_top = jnp.full((1, COLS), -jnp.inf, F32)
    col_sum = jnp.zeros((1, COLS), F32)
    for i in range(ROWS // chunk):
        rows = pl.ds(i * chunk, chunk)
        s = scale * lax.dot_general(
            img[rows, :], txt[...], (((1,), (1,)), ((), ())), preferred_element_type=F32
        )
        scores[rows, :] = s
        out = pltpu.make_async_copy(scores.at[rows], scores_out.at[rows], sem_out.at[2 + i])
        out.start()
        outs.append(out)
        top = jnp.max(s, axis=1, keepdims=True)
        total = jnp.sum(jnp.exp(s - top), axis=1, keepdims=True)
        row_col[rows, :] = jnp.broadcast_to(top + jnp.log(total), (chunk, 128))
        new_top = jnp.maximum(col_top, jnp.max(s, axis=0, keepdims=True))
        col_sum = col_sum * jnp.exp(col_top - new_top) + jnp.sum(
            jnp.exp(s - new_top), axis=0, keepdims=True
        )
        col_top = new_top
    col_out[...] = col_top + jnp.log(col_sum)
    row_out[...] = jnp.transpose(row_col[...])[0:1, :]
    diag_out[...] = jnp.zeros((1, 128), F32)

    @pl.when(has_diagonal(x, y, z))
    def _():
        mask = on_diagonal(x)
        total = jnp.zeros((1, 128), F32)
        for row, col in diagonal_blocks(x, c):
            block = scores[pl.ds(pl.multiple_of(row, SHARD), SHARD), pl.ds(col, 128)]
            total += jnp.sum(jnp.where(mask, block, 0.0), axis=0, keepdims=True)
        diag_out[...] = total

    for copy in outs + [out_img, out_txt]:
        copy.wait()


def weights_kernel(at, scores, row_lse, col_lse, own_out, other_out, row_col):
    x, y, z, c = at[0], at[1], at[2], at[3]
    row_col[...] = jnp.transpose(jnp.broadcast_to(row_lse[...], (128, ROWS)))
    chunk = 128

    def weigh(s, rows, cols):
        return 0.5 * (jnp.exp(s - rows) + jnp.exp(s - cols))

    for half, out in ((1 - c, other_out), (c, own_out)):
        for i in range(CORE_ROWS // chunk):
            rows = pl.ds(pl.multiple_of(half * CORE_ROWS + i * chunk, chunk), chunk)
            out[i * chunk : (i + 1) * chunk, :] = weigh(
                scores[rows, :], row_col[rows, 0:1], col_lse[...]
            ).astype(BF16)

    @pl.when(has_diagonal(x, y, z))
    def _():
        mask = on_diagonal(x).astype(F32)
        for row, col in diagonal_blocks(x, c):
            rows = pl.ds(pl.multiple_of(row, SHARD), SHARD)
            cols = pl.ds(col, 128)
            block = (weigh(scores[rows, cols], row_col[rows, 0:1], col_lse[:, cols]) - mask).astype(BF16)
            half = row // CORE_ROWS
            within = pl.ds(pl.multiple_of(lax.rem(row, CORE_ROWS), SHARD), SHARD)

            @pl.when(half == c)
            def _():
                own_out[within, cols] = block

            @pl.when(half != c)
            def _():
                other_out[within, cols] = block


def text_kernel(at, own, other, img, *refs):
    a_sent, b_sent, a_own, b_own = refs[:3], refs[3:6], refs[6], refs[7]
    total, rounded, sem = refs[8:]
    x, y, z, c = at[0], at[1], at[2], at[3]
    mine = img[pl.ds(pl.multiple_of(c * CORE_ROWS, CORE_ROWS), CORE_ROWS), :]
    theirs = img[pl.ds(pl.multiple_of((1 - c) * CORE_ROWS, CORE_ROWS), CORE_ROWS), :]
    chunk = 256
    for i in range(COLS // chunk):
        cols = slice(i * chunk, (i + 1) * chunk)
        part = lax.dot_general(
            own[:, cols], mine, (((0,), (0,)), ((), ())), preferred_element_type=F32
        ) + lax.dot_general(
            other[:, cols], theirs, (((0,), (0,)), ((), ())), preferred_element_type=F32
        )
        total[cols, :] = part
        rounded[cols, :] = part.astype(BF16)
    copies = []

    def store(src, dst):
        copy = pltpu.make_async_copy(src, dst, sem.at[len(copies)])
        copy.start()
        copies.append(copy)

    def block(dx, dy, shift_rows):
        row = (lax.rem(x + dx, NX) * NY + lax.rem(y + dy, NY)) * SHARD + shift_rows
        return pl.ds(pl.multiple_of(row, HALF), HALF)

    for d in (1, 2, 3):
        for e in range(4):
            place = pl.ds(e * HALF, HALF)
            store(rounded.at[block(e, d, 0)], a_sent[d - 1].at[place])
            store(rounded.at[block(d, e, HALF)], b_sent[d - 1].at[place])
    for e in range(4):
        place = pl.ds(e * HALF, HALF)
        store(total.at[block(e, 0, 0)], a_own.at[place])
        store(total.at[block(0, e, HALF)], b_own.at[place])
    for copy in copies:
        copy.wait()


def image_kernel(at, own, received, txt, other_txt, *refs):
    up, down, up_far, down_far, here, up_two, down_two = refs[:7]
    total, rounded, sem = refs[7:]
    z = at[2]
    chunk = 256
    for i in range(CORE_ROWS // chunk):
        rows = slice(i * chunk, (i + 1) * chunk)
        part = jnp.dot(own[rows, :], txt[...], preferred_element_type=F32) + jnp.dot(
            received[rows, :], other_txt[...], preferred_element_type=F32
        )
        total[rows, :] = part
        rounded[rows, :] = part.astype(BF16)
    copies = []

    def store(src, dst):
        copy = pltpu.make_async_copy(src, dst, sem.at[len(copies)])
        copy.start()
        copies.append(copy)

    def block(dz, start=0, size=SHARD):
        return pl.ds(pl.multiple_of(lax.rem(z + dz + NZ, NZ) * SHARD + start, HALF), size)

    store(rounded.at[block(1)], up.at[pl.ds(0, SHARD)])
    store(rounded.at[block(3)], up.at[pl.ds(SHARD, SHARD)])
    store(rounded.at[block(-1)], down.at[pl.ds(0, SHARD)])
    store(rounded.at[block(-3)], down.at[pl.ds(SHARD, SHARD)])
    store(rounded.at[block(4, 0, HALF)], up_far)
    store(rounded.at[block(4, HALF, HALF)], down_far)
    store(total.at[block(0)], here)
    store(total.at[block(2)], up_two)
    store(total.at[block(-2)], down_two)
    for copy in copies:
        copy.wait()


def shards(image, text):
    embed = image.shape[1]
    scale = 4.0 / math.sqrt(embed)
    me = lax.axis_index(AXES)
    c = lax.rem(me, NC)
    at = jnp.stack([me // (NY * NZ * NC), lax.rem(me // (NZ * NC), NY), lax.rem(me // NC, NZ), c])
    at = at.astype(jnp.int32)

    first, second = text[:HALF], text[HALF:]
    steps = (1, -1, 2)
    a = jnp.concatenate([first] + [shift(first, y=d) for d in steps])
    b = jnp.concatenate([second] + [shift(second, x=d) for d in steps])
    text_in = [a] + [shift(a, x=d) for d in steps] + [b] + [shift(b, y=d) for d in steps]
    partner = swap(image, 3, 1)
    pair = jnp.where(c == 0, jnp.concatenate([image, partner]), jnp.concatenate([partner, image]))
    one = ring_step(pair)
    two = ring_step(one)
    three = ring_step(two)
    four = ring_step(lax.dynamic_slice_in_dim(three, c * SHARD, SHARD))
    image_in = [pair, one, two, three] + [swap(v, 3, 1) for v in (one, two, three)] + [four, swap(four, 3, 1)]

    shape = jax.ShapeDtypeStruct
    tile = 2 * ROWS * COLS * embed
    scores, img, txt, row_part, col_part, diag = call(
        functools.partial(scores_kernel, scale),
        [
            (shape((ROWS, COLS), F32), False),
            (shape((ROWS, embed), BF16), False),
            (shape((COLS, embed), BF16), False),
            (shape((1, ROWS), F32), True),
            (shape((1, COLS), F32), True),
            (shape((1, 128), F32), True),
        ],
        17,
        (),
        [
            pltpu.VMEM((ROWS, embed), BF16),
            pltpu.VMEM((COLS, embed), BF16),
            pltpu.VMEM((ROWS, COLS), F32),
            pltpu.VMEM((ROWS, 128), F32),
            pltpu.SemaphoreType.DMA((48,)),
            pltpu.SemaphoreType.DMA((6,)),
        ],
        tile,
        2 * ROWS * COLS,
        14 << 20,
        at,
        *image_in,
        *text_in,
    )
    other_txt = swap(txt, 3, 1)
    row_lse, col_lse = row_part, col_part
    for (row_axis, row_bit), (col_axis, col_bit) in (
        ((3, 1), (1, 1)),
        ((2, 1), (1, 2)),
        ((2, 2), (0, 1)),
        ((2, 4), (0, 2)),
    ):
        row_lse = merge(row_lse, swap(row_lse, row_axis, row_bit))
        col_lse = merge(col_lse, swap(col_lse, col_axis, col_bit))

    own, other = call(
        weights_kernel,
        [(shape((CORE_ROWS, COLS), BF16), True), (shape((CORE_ROWS, COLS), BF16), True)],
        3,
        (0, 1, 2),
        [pltpu.VMEM((ROWS, 128), F32)],
        8 * ROWS * COLS,
        2 * ROWS * COLS,
        6 << 20,
        at,
        scores,
        row_lse,
        col_lse,
    )
    received = swap(other, 3, 1)
    sent = shape((4 * HALF, embed), BF16)
    kept = shape((4 * HALF, embed), F32)
    *parts, a_own, b_own = call(
        text_kernel,
        [(sent, False)] * 6 + [(kept, False)] * 2,
        3,
        (0, 1, 2),
        [
            pltpu.VMEM((COLS, embed), F32),
            pltpu.VMEM((COLS, embed), BF16),
            pltpu.SemaphoreType.DMA((32,)),
        ],
        tile,
        0,
        8 << 20,
        at,
        own,
        other,
        img,
    )
    a_sum, b_sum = a_own, b_own
    for d in (1, 2, 3):
        a_sum = a_sum + shift(parts[d - 1], y=d).astype(F32)
        b_sum = b_sum + shift(parts[d + 2], x=d).astype(F32)
    up, down, up_far, down_far, here, up_two, down_two = call(
        image_kernel,
        [(shape((2 * SHARD, embed), BF16), False)] * 2
        + [(shape((HALF, embed), BF16), False)] * 2
        + [(shape((SHARD, embed), F32), False)] * 3,
        4,
        (0, 1, 2, 3),
        [
            pltpu.VMEM((CORE_ROWS, embed), F32),
            pltpu.VMEM((CORE_ROWS, embed), BF16),
            pltpu.SemaphoreType.DMA((9,)),
        ],
        tile,
        0,
        10 << 20,
        at,
        own,
        received,
        txt,
        other_txt,
    )
    up, down = shift(up, z=1).astype(F32), shift(down, z=-1).astype(F32)
    up_far, down_far = shift(up_far, z=2).astype(F32), shift(down_far, z=-2).astype(F32)
    up_two = up_two + up[SHARD:] + jnp.pad(up_far, ((0, HALF), (0, 0)))
    down_two = down_two + down[SHARD:] + jnp.pad(down_far, ((HALF, 0), (0, 0)))
    up_two, down_two = shift(up_two.astype(BF16), z=2), shift(down_two.astype(BF16), z=-2)
    image_grad = here + up[:SHARD] + down[:SHARD] + up_two.astype(F32) + down_two.astype(F32)

    first, second = a_sum[:HALF], b_sum[:HALF]
    for d in (1, 2, 3):
        part = slice(d * HALF, (d + 1) * HALF)
        first = first + shift(a_sum[part].astype(BF16), x=d).astype(F32)
        second = second + shift(b_sum[part].astype(BF16), y=d).astype(F32)
    text_grad = jnp.concatenate([first, second])

    loss = jnp.full((1, 128), (0.5 * (jnp.sum(row_lse) + jnp.sum(col_lse)) / 16) - jnp.sum(diag), F32)
    for axis, bit in ((3, 1), (1, 1), (2, 1), (0, 1), (1, 2), (0, 2), (2, 2), (2, 4)):
        loss = loss + swap(loss, axis, bit)
    loss = loss[0, 0] / (ROWS * NX * NY)
    return image_grad.astype(BF16), text_grad.astype(BF16), loss


def solution(mesh):
    return jax.shard_map(
        shards,
        mesh=mesh,
        in_specs=(P(("img", "txt"), None), P(("txt", "img"), None)),
        out_specs=(P(("img", "txt"), None), P(("txt", "img"), None), P()),
        check_vma=False,
    )
```

```python
import functools
import math

import jax
import jax.numpy as jnp
from jax import lax
from jax.experimental import pallas as pl
from jax.experimental.pallas import tpu as pltpu
from jax.sharding import PartitionSpec as P

NX, NY, NZ, NC = 4, 4, 8, 2
AXES = ("img", "txt")
SHARD = 64
HALF = SHARD // 2
ROWS = NZ * SHARD
PLANE = NX * NY * SHARD
COLS = NC * PLANE
NOTE = 16
BF16, F32 = jnp.bfloat16, jnp.float32


def device_id(x, y, z, c):
    return (((x % NX) * NY + y % NY) * NZ + z % NZ) * NC + c % NC


COORDINATES = [(x, y, z, c) for x in range(NX) for y in range(NY) for z in range(NZ) for c in range(NC)]


def shift_z(value, by):
    pairs = [(device_id(x, y, z, c), device_id(x, y, z + by, c)) for x, y, z, c in COORDINATES]
    return lax.ppermute(value, AXES, pairs)


def shift_plane(value, by, first):
    pairs = []
    for x, y, z, c in COORDINATES:
        along_y = (c == 0) == first
        to = (x, y + by) if along_y else (x + by, y)
        pairs.append((device_id(x, y, z, c), device_id(*to, z, c)))
    return lax.ppermute(value, AXES, pairs)


def swap(value, axis, bit):
    pairs = []
    for at in COORDINATES:
        to = list(at)
        to[axis] ^= bit
        pairs.append((device_id(*at), device_id(*to)))
    return lax.ppermute(value, AXES, pairs)


def swap_core(value):
    return swap(value, 3, 1)


def merge(first, second):
    top = jnp.maximum(first, second)
    return top + jnp.log(jnp.exp(first - top) + jnp.exp(second - top))


def merge_columns(first, second):
    lanes = lax.broadcasted_iota(jnp.int32, first.shape, 1)
    return jnp.where(lanes < COLS, merge(first, second), first + second)


def call(kernel, outs, args, scratch, flops, transcendentals, moved, at, vmem_mib):
    vmem = pl.BlockSpec(memory_space=pltpu.VMEM)
    return pl.pallas_call(
        kernel,
        out_shape=[jax.ShapeDtypeStruct(shape, dtype) for shape, dtype in outs],
        in_specs=[pl.BlockSpec(memory_space=pltpu.SMEM)] + [vmem] * len(args),
        out_specs=[vmem] * len(outs),
        scratch_shapes=scratch,
        cost_estimate=pl.CostEstimate(flops=flops, transcendentals=transcendentals, bytes_accessed=moved),
        compiler_params=pltpu.CompilerParams(vmem_limit_bytes=vmem_mib << 20),
    )(at, *args)


def diagonal_blocks(c):
    for zz in range(NZ):
        col = (zz // 4) * PLANE + (zz % 4) * NY * SHARD + c * 2 * SHARD
        yield zz * SHARD, pl.multiple_of(col, 128)


def on_diagonal(x):
    rows = lax.broadcasted_iota(jnp.int32, (SHARD, 128), 0)
    lanes = lax.broadcasted_iota(jnp.int32, (SHARD, 128), 1)
    return lanes == rows + (x // 2) * SHARD


def has_diagonal(x, y, z):
    return z == (x % 2) * 4 + y


def block_row(xx, yy):
    return pl.multiple_of((lax.rem(xx + NX, NX) * NY + lax.rem(yy + NY, NY)) * SHARD, SHARD)


def write_note(ref, value):
    high = value.astype(BF16)
    rest = value - high.astype(F32)
    middle = rest.astype(BF16)
    low = (rest - middle.astype(F32)).astype(BF16)
    for i, term in enumerate((high, middle, low)):
        ref[:, i * 128 : (i + 1) * 128] = jnp.broadcast_to(term.astype(F32), (NOTE, 128)).astype(BF16)
    ref[:, 384:] = jnp.zeros((NOTE, ref.shape[1] - 384), BF16)


def read_note(rows):
    terms = [rows[0:1, i * 128 : (i + 1) * 128].astype(F32) for i in range(3)]
    return terms[0] + terms[1] + terms[2]


STEPS = (0, 1, -1, 2)


def scores_kernel(scale, at, *refs):
    image_in, text_in = refs[:8], refs[8:16]
    scores, img, txt, row_out, col_out, row_top, row_part = refs[16:]
    x, y, z, c = at[0], at[1], at[2], at[3]
    for ref, step in zip(image_in, (0, -1, 1, -2, 2, -3, 3, -4)):
        where = lax.rem(z + step + NZ, NZ) * SHARD
        img[pl.ds(pl.multiple_of(where, SHARD), SHARD), :] = ref[...]
    for own in range(2):
        core = c if own == 0 else 1 - c
        for i, d in enumerate(STEPS):
            for j, e in enumerate(STEPS):
                dx, dy = jnp.where(core == 0, d, e), jnp.where(core == 0, e, d)
                where = pl.multiple_of(core * PLANE + block_row(x - dx, y - dy), SHARD)
                txt[pl.ds(where, SHARD), :] = text_in[own * 4 + i][j * SHARD : (j + 1) * SHARD, :]

    chunk = 512
    row_part[...] = jnp.full((ROWS, 128), -jnp.inf, F32)

    @pl.loop(0, COLS // chunk)
    def _(i):
        cols = pl.ds(pl.multiple_of(i * chunk, chunk), chunk)
        s = scale * lax.dot_general(
            img[...], txt[cols, :], (((1,), (1,)), ((), ())), preferred_element_type=F32
        )
        scores[:, cols] = s
        tops = row_part[...]
        for j in range(chunk // 128):
            tops = jnp.maximum(tops, s[:, j * 128 : (j + 1) * 128])
        row_part[...] = tops
        top = jnp.max(s, axis=0, keepdims=True)
        col_out[:, cols] = top + jnp.log(jnp.sum(jnp.exp(s - top), axis=0, keepdims=True))

    row_top[...] = jnp.broadcast_to(jnp.max(row_part[...], axis=1, keepdims=True), (ROWS, 128))
    row_part[...] = jnp.zeros((ROWS, 128), F32)

    @pl.loop(0, COLS // chunk)
    def _(i):
        for j in range(chunk // 128):
            cols = pl.ds(pl.multiple_of(i * chunk + j * 128, 128), 128)
            row_part[...] += jnp.exp(scores[:, cols] - row_top[...])

    row = row_top[...] + jnp.log(jnp.sum(row_part[...], axis=1, keepdims=True))
    row_out[...] = jnp.transpose(row)[0:1, :]
    col_out[:, COLS:] = jnp.zeros((1, 128), F32)

    @pl.when(has_diagonal(x, y, z))
    def _():
        mask = on_diagonal(x)
        total = jnp.zeros((1, 128), F32)
        for row, col in diagonal_blocks(c):
            block = scores[row : row + SHARD, pl.ds(col, 128)]
            total += jnp.sum(jnp.where(mask, block, 0.0), axis=0, keepdims=True)
        total = jnp.sum(total, axis=1, keepdims=True)
        col_out[:, COLS:] = jnp.broadcast_to(total, (1, 128))


def concat_kernel(at, *refs):
    for i, ref in enumerate(refs[:-1]):
        refs[-1][i * SHARD : (i + 1) * SHARD, :] = ref[...]


def weights_kernel(at, scores, row_lse, col_lse, own_out, other_out, p_out, q_out, row_col):
    x, y, z, c = at[0], at[1], at[2], at[3]
    row_col[...] = jnp.transpose(jnp.broadcast_to(row_lse[...], (128, ROWS)))

    def weigh(s, rows, cols):
        return 0.5 * (jnp.exp(s - rows) + jnp.exp(s - cols))

    chunk = 128
    for half, out in ((1 - c, other_out), (c, own_out)):

        @pl.loop(0, PLANE // chunk)
        def _(i, half=half, out=out):
            cols = pl.ds(pl.multiple_of(half * PLANE + i * chunk, chunk), chunk)
            out[:, pl.ds(pl.multiple_of(i * chunk, chunk), chunk)] = weigh(
                scores[:, cols], row_col[...], col_lse[:, cols]
            ).astype(BF16)

    @pl.when(has_diagonal(x, y, z))
    def _():
        mask = on_diagonal(x).astype(F32)
        for zz, (row, col) in enumerate(diagonal_blocks(c)):
            rows, cols = pl.ds(row, SHARD), pl.ds(col, 128)
            block = (weigh(scores[rows, cols], row_col[rows, :], col_lse[:, cols]) - mask).astype(BF16)
            core = zz // 4
            within = pl.ds(pl.multiple_of(col - core * PLANE, 128), 128)

            @pl.when(c == core)
            def _():
                own_out[rows, within] = block

            @pl.when(c != core)
            def _():
                other_out[rows, within] = block

    row_sum = 0.5 * jnp.sum(row_lse[...], axis=1, keepdims=True)
    p_out[...] = jnp.broadcast_to(row_sum, (1, 128))
    col_sum = 0.5 * jnp.sum(col_lse[:, :COLS], axis=1, keepdims=True)
    q_out[...] = jnp.broadcast_to(col_sum, (1, 128)) - col_lse[:, COLS:]


def image_kernel(at, own, other, txt, q, *refs):
    up, down, up_far, down_far, here, up_two, down_two = refs[:7]
    total = refs[7]
    z, c = at[2], at[3]
    mine = pl.ds(pl.multiple_of(c * PLANE, PLANE), PLANE)
    theirs = pl.ds(pl.multiple_of((1 - c) * PLANE, PLANE), PLANE)
    chunk = 256

    @pl.loop(0, total.shape[1] // chunk)
    def _(i):
        cols = pl.ds(pl.multiple_of(i * chunk, chunk), chunk)
        total[:, cols] = jnp.dot(own[...], txt[mine, cols], preferred_element_type=F32) + jnp.dot(
            other[...], txt[theirs, cols], preferred_element_type=F32
        )

    def block(dz, start=0, size=SHARD):
        return total[pl.ds(pl.multiple_of(lax.rem(z + dz + NZ, NZ) * SHARD + start, HALF), size), :]

    up[:SHARD] = block(1).astype(BF16)
    up[SHARD : 2 * SHARD] = block(3).astype(BF16)
    down[:SHARD] = block(-1).astype(BF16)
    down[SHARD : 2 * SHARD] = block(-3).astype(BF16)
    up_far[:HALF] = block(4, 0, HALF).astype(BF16)
    down_far[:HALF] = block(4, HALF, HALF).astype(BF16)
    here[...] = block(0)
    up_two[...] = block(2)
    down_two[...] = block(-2)
    for ref in (up, down):
        write_note(ref.at[2 * SHARD :], q[...])
    for ref in (up_far, down_far):
        write_note(ref.at[HALF:], q[...])


def text_kernel(at, own, received, img, img_other, p_own, p_other, *refs):
    sent, kept, p_out = refs[:3], refs[3], refs[4]
    total = refs[5]
    x, y, c = at[0], at[1], at[3]
    p = p_own[...] + p_other[...]
    p_out[...] = p
    chunk = 256

    @pl.loop(0, PLANE // chunk)
    def _(i):
        cols = pl.ds(pl.multiple_of(i * chunk, chunk), chunk)
        total[cols, :] = lax.dot_general(
            own[:, cols], img[...], (((0,), (0,)), ((), ())), preferred_element_type=F32
        ) + lax.dot_general(
            received[:, cols], img_other[...], (((0,), (0,)), ((), ())), preferred_element_type=F32
        )

    for d in range(4):
        for e in range(4):
            dx, dy = jnp.where(c == 0, e, d), jnp.where(c == 0, d, e)
            part = total[pl.ds(block_row(x + dx, y + dy), SHARD), :]
            place = slice(e * SHARD, (e + 1) * SHARD)
            if d == 0:
                kept[place] = part
            else:
                sent[d - 1][place] = part.astype(BF16)
        if d:
            write_note(sent[d - 1].at[4 * SHARD :], p)


def image_middle_kernel(at, up, down, up_far, down_far, here, up_two, down_two, q, up_out, down_out, here_out, q_out):
    near, far = slice(0, SHARD), slice(SHARD, 2 * SHARD)
    here_out[...] = here[...] + up[near].astype(F32) + down[near].astype(F32)
    low, high = slice(0, HALF), slice(HALF, SHARD)
    above, below = up_two[...] + up[far].astype(F32), down_two[...] + down[far].astype(F32)
    up_out[low] = (above[low] + up_far[low].astype(F32)).astype(BF16)
    up_out[high] = above[high].astype(BF16)
    down_out[low] = below[low].astype(BF16)
    down_out[high] = (below[high] + down_far[low].astype(F32)).astype(BF16)
    note_up, note_down = read_note(up[2 * SHARD :]), read_note(down[2 * SHARD :])
    write_note(up_out.at[SHARD:], q[...] + note_up + read_note(up_far[HALF:]))
    write_note(down_out.at[SHARD:], q[...] + note_down)
    q_out[...] = q[...] + note_up + note_down


def text_middle_kernel(at, first, second, third, kept, p, *refs):
    sent, kept_out, p_out = refs[:3], refs[3], refs[4]
    total = p[...] + read_note(first[4 * SHARD :]) + read_note(second[4 * SHARD :]) + read_note(third[4 * SHARD :])
    p_out[...] = total
    for e in range(4):
        rows = slice(e * SHARD, (e + 1) * SHARD)
        part = kept[rows] + first[rows].astype(F32) + second[rows].astype(F32) + third[rows].astype(F32)
        if e == 0:
            kept_out[...] = part
        else:
            sent[e - 1][:SHARD] = part.astype(BF16)
            write_note(sent[e - 1].at[SHARD:], total)


def last_kernel(at, up, down, here, q, first, second, third, kept, p, image_out, text_out, loss_out):
    body = slice(0, SHARD)
    image_out[...] = (here[...] + up[body].astype(F32) + down[body].astype(F32)).astype(BF16)
    text = kept[...] + first[body].astype(F32) + second[body].astype(F32) + third[body].astype(F32)
    text_out[...] = text.astype(BF16)
    loss = q[...] + p[...]
    for message in (up, down, first, second, third):
        loss += read_note(message[SHARD:])
    loss_out[...] = loss / (ROWS * NC * NX * NY)


def shards(image, text):
    embed = image.shape[1]
    scale = 4.0 / math.sqrt(embed)
    me = lax.axis_index(AXES)
    at = jnp.stack([me // (NY * NZ * NC), lax.rem(me // (NZ * NC), NY), lax.rem(me // NC, NZ), lax.rem(me, NC)])
    at = at.astype(jnp.int32)

    up, down = shift_z(image, 1), shift_z(image, -1)
    near = [shift_plane(text, d, True) for d in STEPS[1:]]
    up, down, *near = lax.optimization_barrier((up, down, *near))
    (line,) = call(concat_kernel, [((4 * SHARD, embed), BF16)], [text, *near], [], 0, 0, 1 << 20, at, 4)
    far = [shift_plane(line, d, False) for d in STEPS[1:]]
    image_in = [image, up, down]
    up, down = lax.optimization_barrier((shift_z(up, 1), shift_z(down, -1)))
    image_in += [up, down]
    up, down, *far = lax.optimization_barrier((shift_z(up, 1), shift_z(down, -1), *far))
    image_in += [up, down]
    image_in.append(shift_z(up, 1))
    text_in = [line, *far]
    text_in += [swap_core(part) for part in text_in]

    tile = 2 * ROWS * COLS * embed
    scores, img, txt, row_lse, col_lse = call(
        functools.partial(scores_kernel, scale),
        [
            ((ROWS, COLS), F32),
            ((ROWS, embed), BF16),
            ((COLS, embed), BF16),
            ((1, ROWS), F32),
            ((1, COLS + 128), F32),
        ],
        image_in + text_in,
        [pltpu.VMEM((ROWS, 128), F32), pltpu.VMEM((ROWS, 128), F32)],
        tile,
        2 * ROWS * COLS,
        14 << 20,
        at,
        16,
    )
    img_other = swap_core(img)
    col_lse = merge_columns(col_lse, swap_core(col_lse))
    for axis, bit in ((1, 1), (1, 2), (0, 1), (0, 2)):
        col_lse = merge_columns(col_lse, swap(col_lse, axis, bit))
    for bit in (1, 2, 4):
        row_lse = merge(row_lse, swap(row_lse, 2, bit))

    half = ((ROWS, PLANE), BF16)
    scalar = ((1, 128), F32)
    own, other, p, q = call(
        weights_kernel,
        [half, half, scalar, scalar],
        (scores, row_lse, col_lse),
        [pltpu.VMEM((ROWS, 128), F32)],
        8 * ROWS * COLS,
        2 * ROWS * COLS,
        6 << 20,
        at,
        12,
    )
    received = swap_core(other)
    p_other = swap_core(p)
    message = lambda rows: ((rows + NOTE, embed), BF16)
    up, down, up_far, down_far, here, up_two, down_two = call(
        image_kernel,
        [message(2 * SHARD)] * 2 + [message(HALF)] * 2 + [((SHARD, embed), F32)] * 3,
        (own, other, txt, q),
        [pltpu.VMEM((ROWS, embed), F32)],
        tile,
        0,
        10 << 20,
        at,
        16,
    )
    received, here = lax.optimization_barrier((received, here))
    *sent, kept, p = call(
        text_kernel,
        [message(4 * SHARD)] * 3 + [((4 * SHARD, embed), F32), scalar],
        (own, received, img, img_other, p, p_other),
        [pltpu.VMEM((PLANE, embed), F32)],
        tile,
        0,
        8 << 20,
        at,
        20,
    )
    up, down = shift_z(up, 1), shift_z(down, -1)
    up_far, down_far = shift_z(up_far, 2), shift_z(down_far, -2)
    sent = [shift_plane(part, d, True) for d, part in enumerate(sent, 1)]
    up, down, here, q = call(
        image_middle_kernel,
        [message(SHARD)] * 2 + [((SHARD, embed), F32), scalar],
        (up, down, up_far, down_far, here, up_two, down_two, q),
        [],
        1 << 20,
        0,
        2 << 20,
        at,
        12,
    )
    up, down = shift_z(up, 2), shift_z(down, -2)
    *sent, kept, p = call(
        text_middle_kernel,
        [message(SHARD)] * 3 + [((SHARD, embed), F32), scalar],
        (*sent, kept, p),
        [],
        1 << 20,
        0,
        4 << 20,
        at,
        12,
    )
    sent = [shift_plane(part, d, False) for d, part in enumerate(sent, 1)]
    image_grad, text_grad, loss = call(
        last_kernel,
        [((SHARD, embed), BF16)] * 2 + [scalar],
        (up, down, here, q, *sent, kept, p),
        [],
        1 << 20,
        0,
        2 << 20,
        at,
        12,
    )
    return image_grad, text_grad, loss[0, 0]


def solution(mesh):
    return jax.shard_map(
        shards,
        mesh=mesh,
        in_specs=(P(("img", "txt"), None), P(("txt", "img"), None)),
        out_specs=(P(("img", "txt"), None), P(("txt", "img"), None), P()),
        check_vma=False,
    )
```

```python
import functools
import math

import jax
import jax.numpy as jnp
from jax import lax
from jax.experimental import pallas as pl
from jax.experimental.pallas import tpu as pltpu
from jax.sharding import PartitionSpec as P

NX, NY, NZ, NC = 4, 4, 8, 2
AXES = ("img", "txt")
SHARD = 64
HALF = SHARD // 2
ROWS = NZ * SHARD
PLANE = NX * NY * SHARD
COLS = NC * PLANE
NOTE = 16
BF16, F32 = jnp.bfloat16, jnp.float32


def device_id(x, y, z, c):
    return (((x % NX) * NY + y % NY) * NZ + z % NZ) * NC + c % NC


COORDINATES = [(x, y, z, c) for x in range(NX) for y in range(NY) for z in range(NZ) for c in range(NC)]


def shift_z(value, by):
    pairs = [(device_id(x, y, z, c), device_id(x, y, z + by, c)) for x, y, z, c in COORDINATES]
    return lax.ppermute(value, AXES, pairs)


def shift_plane(value, by, first):
    pairs = []
    for x, y, z, c in COORDINATES:
        along_y = (c == 0) == first
        to = (x, y + by) if along_y else (x + by, y)
        pairs.append((device_id(x, y, z, c), device_id(*to, z, c)))
    return lax.ppermute(value, AXES, pairs)


def shift_far(value):
    pairs = [(device_id(x, y, z, c), device_id(x, y, z + 2 - 4 * c, c)) for x, y, z, c in COORDINATES]
    return lax.ppermute(value, AXES, pairs)


def swap(value, axis, bit):
    pairs = []
    for at in COORDINATES:
        to = list(at)
        to[axis] ^= bit
        pairs.append((device_id(*at), device_id(*to)))
    return lax.ppermute(value, AXES, pairs)


def swap_core(value):
    return swap(value, 3, 1)


def merge(*parts):
    top = functools.reduce(jnp.maximum, parts)
    return top + jnp.log(sum(jnp.exp(part - top) for part in parts))


def merge_columns(*parts):
    lanes = lax.broadcasted_iota(jnp.int32, parts[0].shape, 1)
    return jnp.where(lanes < COLS, merge(*parts), sum(parts))


def shift_one(value, axis, by):
    pairs = []
    for at in COORDINATES:
        to = list(at)
        to[axis] += by
        pairs.append((device_id(*at), device_id(*to)))
    return lax.ppermute(value, AXES, pairs)


def position():
    img, txt = lax.axis_index("img"), lax.axis_index("txt")
    y = lax.rem(img, 2) * 2 + txt // (NZ * NC)
    return img // 2, y, lax.rem(txt // NC, NZ), lax.rem(txt, NC)


def call(kernel, outs, args, scratch, flops, transcendentals, moved, vmem_mib):
    vmem = pl.BlockSpec(memory_space=pltpu.VMEM)
    return pl.pallas_call(
        lambda *refs: kernel(position(), *refs),
        out_shape=[jax.ShapeDtypeStruct(shape, dtype) for shape, dtype in outs],
        in_specs=[vmem] * len(args),
        out_specs=[vmem] * len(outs),
        scratch_shapes=scratch,
        cost_estimate=pl.CostEstimate(flops=flops, transcendentals=transcendentals, bytes_accessed=moved),
        compiler_params=pltpu.CompilerParams(vmem_limit_bytes=vmem_mib << 20),
    )(*args)


def diagonal_blocks(c):
    for zz in range(NZ):
        col = (zz // 4) * PLANE + (zz % 4) * NY * SHARD + c * 2 * SHARD
        yield zz * SHARD, pl.multiple_of(col, 128)


def on_diagonal(x):
    rows = lax.broadcasted_iota(jnp.int32, (SHARD, 128), 0)
    lanes = lax.broadcasted_iota(jnp.int32, (SHARD, 128), 1)
    return lanes == rows + (x // 2) * SHARD


def has_diagonal(x, y, z):
    return z == (x % 2) * 4 + y


def block_row(xx, yy):
    return pl.multiple_of((lax.rem(xx + NX, NX) * NY + lax.rem(yy + NY, NY)) * SHARD, SHARD)


def write_note(ref, value):
    high = value.astype(BF16).astype(F32)
    middle = (value - high).astype(BF16).astype(F32)
    low = value - high - middle
    which = lax.broadcasted_iota(jnp.int32, (NOTE, 128), 0)
    rows = jnp.where(which == 0, high, jnp.where(which == 1, middle, jnp.where(which == 2, low, 0.0)))
    ref[ref.shape[0] - NOTE :, :] = rows.astype(BF16)


def read_note(ref):
    terms = [ref[ref.shape[0] - NOTE + i : ref.shape[0] - NOTE + i + 1, :].astype(F32) for i in range(3)]
    return terms[0] + terms[1] + terms[2]


def part_of(ref, index, strip, strips):
    start = (index * strips + strip) * SHARD
    return slice(start, start + SHARD)


def columns(strip):
    return slice(strip * 128, (strip + 1) * 128)


STEPS = (0, 1, -1, 2)


def scores_kernel(scale, at, *refs):
    image_in, text_in = refs[:8], refs[8:16]
    scores, img, txt, row_out, col_out, row_top, row_part = refs[16:]
    x, y, z, c = at[0], at[1], at[2], at[3]
    for ref, step in zip(image_in, (0, -1, 1, -2, 2, -3, 3, -4)):
        where = lax.rem(z + step + NZ, NZ) * SHARD
        img[pl.ds(pl.multiple_of(where, SHARD), SHARD), :] = ref[...]
    for own in range(2):
        core = c if own == 0 else 1 - c
        for i, d in enumerate(STEPS):
            for j, e in enumerate(STEPS):
                dx, dy = jnp.where(core == 0, d, e), jnp.where(core == 0, e, d)
                where = pl.multiple_of(core * PLANE + block_row(x - dx, y - dy), SHARD)
                txt[pl.ds(where, SHARD), :] = text_in[own * 4 + i][j * SHARD : (j + 1) * SHARD, :]

    chunk = 512
    row_part[...] = jnp.full((ROWS, 128), -jnp.inf, F32)

    @pl.loop(0, COLS // chunk)
    def _(i):
        cols = pl.ds(pl.multiple_of(i * chunk, chunk), chunk)
        s = scale * lax.dot_general(
            img[...], txt[cols, :], (((1,), (1,)), ((), ())), preferred_element_type=F32
        )
        scores[:, cols] = s
        tops = row_part[...]
        for j in range(chunk // 128):
            tops = jnp.maximum(tops, s[:, j * 128 : (j + 1) * 128])
        row_part[...] = tops
        top = jnp.max(s, axis=0, keepdims=True)
        col_out[:, cols] = top + jnp.log(jnp.sum(jnp.exp(s - top), axis=0, keepdims=True))

    row_top[...] = jnp.broadcast_to(jnp.max(row_part[...], axis=1, keepdims=True), (ROWS, 128))
    row_part[...] = jnp.zeros((ROWS, 128), F32)

    @pl.loop(0, COLS // chunk)
    def _(i):
        for j in range(chunk // 128):
            cols = pl.ds(pl.multiple_of(i * chunk + j * 128, 128), 128)
            row_part[...] += jnp.exp(scores[:, cols] - row_top[...])

    row = row_top[...] + jnp.log(jnp.sum(row_part[...], axis=1, keepdims=True))
    row_out[...] = jnp.transpose(row)[0:1, :]
    col_out[:, COLS:] = jnp.zeros((1, 128), F32)

    @pl.when(has_diagonal(x, y, z))
    def _():
        mask = on_diagonal(x)
        total = jnp.zeros((1, 128), F32)
        for row, col in diagonal_blocks(c):
            block = scores[row : row + SHARD, pl.ds(col, 128)]
            total += jnp.sum(jnp.where(mask, block, 0.0), axis=0, keepdims=True)
        total = jnp.sum(total, axis=1, keepdims=True)
        col_out[:, COLS:] = jnp.broadcast_to(total, (1, 128))


def line_kernel(text, *refs):
    near, line, sem = refs[:3], refs[3], refs[4]
    copy = pltpu.make_async_copy(text, line.at[pl.ds(0, SHARD)], sem)
    copy.start()
    for i, ref in enumerate(near, 1):
        line[i * SHARD : (i + 1) * SHARD, :] = ref[...]
    copy.wait()


def weights_kernel(own, at, scores, row_lse, col_lse, out, *refs):
    x, y, z, c = at
    sums, row_col = refs[:-1], refs[-1]
    row_col[...] = jnp.transpose(jnp.broadcast_to(row_lse[...], (128, ROWS)))
    half = c if own else 1 - c

    def weigh(s, rows, cols):
        return 0.5 * (jnp.exp(s - rows) + jnp.exp(s - cols))

    chunk = 128

    @pl.loop(0, PLANE // chunk)
    def _(i):
        cols = pl.ds(pl.multiple_of(half * PLANE + i * chunk, chunk), chunk)
        out[:, pl.ds(pl.multiple_of(i * chunk, chunk), chunk)] = weigh(
            scores[:, cols], row_col[...], col_lse[:, cols]
        ).astype(BF16)

    @pl.when(has_diagonal(x, y, z))
    def _():
        mask = on_diagonal(x).astype(F32)
        for zz, (row, col) in enumerate(diagonal_blocks(c)):
            core = zz // 4

            @pl.when(half == core)
            def _(row=row, col=col, core=core):
                rows, cols = pl.ds(row, SHARD), pl.ds(col, 128)
                block = weigh(scores[rows, cols], row_col[rows, :], col_lse[:, cols]) - mask
                out[rows, pl.ds(pl.multiple_of(col - core * PLANE, 128), 128)] = block.astype(BF16)

    if own:
        p_out, q_out = sums
        row_sum = 0.5 * jnp.sum(row_lse[...], axis=1, keepdims=True)
        p_out[...] = jnp.broadcast_to(row_sum, (1, 128))
        col_sum = 0.5 * jnp.sum(col_lse[:, :COLS], axis=1, keepdims=True)
        q_out[...] = jnp.broadcast_to(col_sum, (1, 128)) - col_lse[:, COLS:]


def image_kernel(at, own, other, txt, q, up, down, far, here, up_two, down_two, total):
    _, _, z, c = at
    mine = pl.ds(pl.multiple_of(c * PLANE, PLANE), PLANE)
    theirs = pl.ds(pl.multiple_of((1 - c) * PLANE, PLANE), PLANE)
    chunk = 256

    @pl.loop(0, total.shape[1] // chunk)
    def _(i):
        cols = pl.ds(pl.multiple_of(i * chunk, chunk), chunk)
        total[:, cols] = jnp.dot(own[...], txt[mine, cols], preferred_element_type=F32) + jnp.dot(
            other[...], txt[theirs, cols], preferred_element_type=F32
        )

    strips = total.shape[1] // 128

    def block(dz, strip):
        return total[pl.ds(pl.multiple_of(lax.rem(z + dz + NZ, NZ) * SHARD, SHARD), SHARD), columns(strip)]

    for i in range(strips):
        for ref, index, dz in ((up, 0, 1), (up, 1, 3), (down, 0, -1), (down, 1, -3), (far, 0, 4)):
            ref[part_of(ref, index, i, strips), :] = block(dz, i).astype(BF16)
        for ref, dz in ((here, 0), (up_two, 2), (down_two, -2)):
            ref[:, columns(i)] = block(dz, i)
    for ref in (up, down, far):
        write_note(ref, q[...])


def text_kernel(at, own, received, img, img_other, p_own, p_other, *refs):
    sent, kept, p_out, total = refs[:3], refs[3], refs[4], refs[5]
    x, y, _, c = at
    p = p_own[...] + p_other[...]
    p_out[...] = p
    chunk = 256

    @pl.loop(0, PLANE // chunk)
    def _(i):
        cols = pl.ds(pl.multiple_of(i * chunk, chunk), chunk)
        total[cols, :] = lax.dot_general(
            own[:, cols], img[...], (((0,), (0,)), ((), ())), preferred_element_type=F32
        ) + lax.dot_general(
            received[:, cols], img_other[...], (((0,), (0,)), ((), ())), preferred_element_type=F32
        )

    strips = total.shape[1] // 128
    for d in range(4):
        for e in range(4):
            dx, dy = jnp.where(c == 0, e, d), jnp.where(c == 0, d, e)
            rows = pl.ds(block_row(x + dx, y + dy), SHARD)
            for i in range(strips):
                part = total[rows, columns(i)]
                if d == 0:
                    kept[e * SHARD : (e + 1) * SHARD, columns(i)] = part
                else:
                    sent[d - 1][part_of(sent[d - 1], e, i, strips), :] = part.astype(BF16)
        if d:
            write_note(sent[d - 1], p)


def image_middle_kernel(at, up, down, far, here, up_two, down_two, q, up_out, down_out, here_out, q_out):
    first_core = at[3] == 0
    strips = here.shape[1] // 128
    for i in range(strips):
        near, rest, cols = part_of(up, 0, i, strips), part_of(up, 1, i, strips), columns(i)
        here_out[:, cols] = here[:, cols] + up[near, :].astype(F32) + down[near, :].astype(F32)
        far_rows = far[near, :].astype(F32)
        above = up_two[:, cols] + up[rest, :].astype(F32) + jnp.where(first_core, far_rows, 0.0)
        below = down_two[:, cols] + down[rest, :].astype(F32) + jnp.where(first_core, 0.0, far_rows)
        up_out[near, :] = above.astype(BF16)
        down_out[near, :] = below.astype(BF16)
    note_up, note_down, note_far = read_note(up), read_note(down), read_note(far)
    write_note(up_out, q[...] + note_up + jnp.where(first_core, note_far, 0.0))
    write_note(down_out, q[...] + note_down + jnp.where(first_core, 0.0, note_far))
    q_out[...] = q[...] + note_up + note_down


def text_middle_kernel(at, first, second, third, kept, p, *refs):
    sent, kept_out, p_out = refs[:3], refs[3], refs[4]
    total = p[...] + read_note(first) + read_note(second) + read_note(third)
    p_out[...] = total
    strips = kept.shape[1] // 128
    for e in range(4):
        for i in range(strips):
            rows, cols = part_of(first, e, i, strips), columns(i)
            part = kept[e * SHARD : (e + 1) * SHARD, cols] + first[rows, :].astype(F32)
            part += second[rows, :].astype(F32) + third[rows, :].astype(F32)
            if e == 0:
                kept_out[:, cols] = part
            else:
                sent[e - 1][part_of(first, 0, i, strips), :] = part.astype(BF16)
        if e:
            write_note(sent[e - 1], total)


def last_kernel(at, up, down, here, q, first, second, third, kept, p, image_out, text_out, loss_out):
    strips = kept.shape[1] // 128
    for i in range(strips):
        rows, cols = part_of(up, 0, i, strips), columns(i)
        image = here[:, cols] + up[rows, :].astype(F32) + down[rows, :].astype(F32)
        image_out[:, cols] = image.astype(BF16)
        text = kept[:, cols] + first[rows, :].astype(F32) + second[rows, :].astype(F32) + third[rows, :].astype(F32)
        text_out[:, cols] = text.astype(BF16)
    loss = q[...] + p[...]
    for message in (up, down, first, second, third):
        loss += read_note(message)
    loss_out[...] = loss / (ROWS * NC * NX * NY)


def shards(image, text):
    embed = image.shape[1]
    scale = 4.0 / math.sqrt(embed)
    up, down = shift_z(image, 1), shift_z(image, -1)
    near = [shift_plane(text, d, True) for d in STEPS[1:]]
    line = pl.pallas_call(
        line_kernel,
        out_shape=jax.ShapeDtypeStruct((4 * SHARD, embed), BF16),
        in_specs=[pl.BlockSpec(memory_space=pltpu.HBM)] + [pl.BlockSpec(memory_space=pltpu.VMEM)] * 3,
        out_specs=pl.BlockSpec(memory_space=pltpu.VMEM),
        scratch_shapes=[pltpu.SemaphoreType.DMA],
        cost_estimate=pl.CostEstimate(flops=0, transcendentals=0, bytes_accessed=1 << 20),
        compiler_params=pltpu.CompilerParams(vmem_limit_bytes=4 << 20),
    )(text, *near)
    image_in = [image, up, down]
    up, down, line = lax.optimization_barrier((shift_z(up, 1), shift_z(down, -1), line))
    image_in += [up, down]
    far = [shift_plane(line, d, False) for d in STEPS[1:]]
    up, down = lax.optimization_barrier((shift_z(up, 1), shift_z(down, -1)))
    image_in += [up, down]
    last, line, *far = lax.optimization_barrier((shift_z(up, 1), line, *far))
    image_in.append(last)
    text_in = [line, *far]
    text_in += [swap_core(part) for part in text_in]

    tile = 2 * ROWS * COLS * embed
    scores, img, txt, row_lse, col_lse = call(
        functools.partial(scores_kernel, scale),
        [
            ((ROWS, COLS), F32),
            ((ROWS, embed), BF16),
            ((COLS, embed), BF16),
            ((1, ROWS), F32),
            ((1, COLS + 128), F32),
        ],
        image_in + text_in,
        [pltpu.VMEM((ROWS, 128), F32), pltpu.VMEM((ROWS, 128), F32)],
        tile,
        2 * ROWS * COLS,
        14 << 20,
        16,
    )
    img_other = swap_core(img)
    col_lse = merge_columns(col_lse, swap_core(col_lse))
    for axis in (1, 0):
        col_lse = merge_columns(col_lse, *[shift_one(col_lse, axis, by) for by in STEPS[1:]])
    for bit in (1, 2, 4):
        row_lse = merge(row_lse, swap(row_lse, 2, bit))

    half = ((ROWS, PLANE), BF16)
    scalar = ((1, 128), F32)
    weights = lambda own, outs, scores: call(
        functools.partial(weights_kernel, own),
        [half, *outs],
        (scores, row_lse, col_lse),
        [pltpu.VMEM((ROWS, 128), F32)],
        4 * ROWS * COLS,
        ROWS * COLS,
        3 << 20,
        12,
    )
    (other,) = weights(False, [], scores)
    scores, other = lax.optimization_barrier((scores, other))
    received = swap_core(other)
    own, p, q = weights(True, [scalar, scalar], scores)
    p_other = swap_core(p)
    message = lambda rows: ((rows * embed // 128 + NOTE, 128), BF16)
    *sent, kept, p = call(
        text_kernel,
        [message(4 * SHARD)] * 3 + [((4 * SHARD, embed), F32), scalar],
        (own, received, img, img_other, p, p_other),
        [pltpu.VMEM((PLANE, embed), F32)],
        tile // 2,
        0,
        12 << 20,
        24,
    )
    other, kept = lax.optimization_barrier((other, kept))
    up, down, far, here, up_two, down_two = call(
        image_kernel,
        [message(2 * SHARD)] * 2 + [message(SHARD)] + [((SHARD, embed), F32)] * 3,
        (own, other, txt, q),
        [pltpu.VMEM((ROWS, embed), F32)],
        tile,
        0,
        10 << 20,
        16,
    )
    up, down = shift_z(up, 1), shift_z(down, -1)
    sent = [shift_plane(part, d, True) for d, part in enumerate(sent, 1)]
    far, sent[0] = lax.optimization_barrier((far, sent[0]))
    far = shift_far(far)
    up, down, here, q = call(
        image_middle_kernel,
        [message(SHARD)] * 2 + [((SHARD, embed), F32), scalar],
        (up, down, far, here, up_two, down_two, q),
        [],
        1 << 20,
        0,
        2 << 20,
        12,
    )
    up, down = shift_z(up, 2), shift_z(down, -2)
    *sent, kept, p = call(
        text_middle_kernel,
        [message(SHARD)] * 3 + [((SHARD, embed), F32), scalar],
        (*sent, kept, p),
        [],
        1 << 20,
        0,
        4 << 20,
        12,
    )
    sent = [shift_plane(part, d, False) for d, part in enumerate(sent, 1)]
    image_grad, text_grad, loss = call(
        last_kernel,
        [((SHARD, embed), BF16)] * 2 + [scalar],
        (up, down, here, q, *sent, kept, p),
        [],
        1 << 20,
        0,
        2 << 20,
        12,
    )
    return image_grad, text_grad, loss[0, 0]


def solution(mesh):
    return jax.shard_map(
        shards,
        mesh=mesh,
        in_specs=(P(("img", "txt"), None), P(("txt", "img"), None)),
        out_specs=(P(("img", "txt"), None), P(("txt", "img"), None), P()),
        check_vma=False,
    )
```

```python
import functools
import math

import jax
import jax.numpy as jnp
from jax import lax
from jax.experimental import pallas as pl
from jax.experimental.pallas import tpu as pltpu
from jax.sharding import PartitionSpec as P

NX, NY, NZ, NC = 4, 4, 8, 2
AXES = ("img", "txt")
SHARD = 64
HALF = SHARD // 2
ROWS = NZ * SHARD
PLANE = NX * NY * SHARD
COLS = NC * PLANE
NOTE = 16
BF16, F32 = jnp.bfloat16, jnp.float32


def device_id(x, y, z, c):
    return (((x % NX) * NY + y % NY) * NZ + z % NZ) * NC + c % NC


COORDINATES = [(x, y, z, c) for x in range(NX) for y in range(NY) for z in range(NZ) for c in range(NC)]


def shift_z(value, by):
    pairs = [(device_id(x, y, z, c), device_id(x, y, z + by, c)) for x, y, z, c in COORDINATES]
    return lax.ppermute(value, AXES, pairs)


def shift_plane(value, by, first):
    pairs = []
    for x, y, z, c in COORDINATES:
        along_y = (c == 0) == first
        to = (x, y + by) if along_y else (x + by, y)
        pairs.append((device_id(x, y, z, c), device_id(*to, z, c)))
    return lax.ppermute(value, AXES, pairs)


def shift_far(value):
    pairs = [(device_id(x, y, z, c), device_id(x, y, z + 2 - 4 * c, c)) for x, y, z, c in COORDINATES]
    return lax.ppermute(value, AXES, pairs)


def swap(value, axis, bit):
    pairs = []
    for at in COORDINATES:
        to = list(at)
        to[axis] ^= bit
        pairs.append((device_id(*at), device_id(*to)))
    return lax.ppermute(value, AXES, pairs)


def swap_core(value):
    return swap(value, 3, 1)


def merge(*parts):
    top = functools.reduce(jnp.maximum, parts)
    return top + jnp.log(sum(jnp.exp(part - top) for part in parts))


def merge_columns(*parts):
    lanes = lax.broadcasted_iota(jnp.int32, parts[0].shape, 1)
    return jnp.where(lanes < COLS, merge(*parts), sum(parts))


def shift_one(value, axis, by):
    pairs = []
    for at in COORDINATES:
        to = list(at)
        to[axis] += by
        pairs.append((device_id(*at), device_id(*to)))
    return lax.ppermute(value, AXES, pairs)


def position():
    img, txt = lax.axis_index("img"), lax.axis_index("txt")
    y = lax.rem(img, 2) * 2 + txt // (NZ * NC)
    return img // 2, y, lax.rem(txt // NC, NZ), lax.rem(txt, NC)


def call(kernel, outs, args, scratch, flops, transcendentals, moved, vmem_mib):
    vmem = pl.BlockSpec(memory_space=pltpu.VMEM)
    return pl.pallas_call(
        lambda *refs: kernel(position(), *refs),
        out_shape=[jax.ShapeDtypeStruct(shape, dtype) for shape, dtype in outs],
        in_specs=[vmem] * len(args),
        out_specs=[vmem] * len(outs),
        scratch_shapes=scratch,
        cost_estimate=pl.CostEstimate(flops=8 * flops, transcendentals=transcendentals, bytes_accessed=moved),
        compiler_params=pltpu.CompilerParams(vmem_limit_bytes=vmem_mib << 20),
    )(*args)


def diagonal_blocks(c):
    for zz in range(NZ):
        yield zz // 4, zz * SHARD, pl.multiple_of((zz % 4) * NY * SHARD + c * 2 * SHARD, 128)


def on_diagonal(x):
    rows = lax.broadcasted_iota(jnp.int32, (SHARD, 128), 0)
    lanes = lax.broadcasted_iota(jnp.int32, (SHARD, 128), 1)
    return lanes == rows + (x // 2) * SHARD


def has_diagonal(x, y, z):
    return z == (x % 2) * 4 + y


def block_row(xx, yy):
    return pl.multiple_of((lax.rem(xx + NX, NX) * NY + lax.rem(yy + NY, NY)) * SHARD, SHARD)


def write_note(ref, value):
    high = value.astype(BF16).astype(F32)
    middle = (value - high).astype(BF16).astype(F32)
    low = value - high - middle
    which = lax.broadcasted_iota(jnp.int32, (NOTE, 128), 0)
    rows = jnp.where(which == 0, high, jnp.where(which == 1, middle, jnp.where(which == 2, low, 0.0)))
    ref[ref.shape[0] - NOTE :, :] = rows.astype(BF16)


def read_note(ref):
    terms = [ref[ref.shape[0] - NOTE + i : ref.shape[0] - NOTE + i + 1, :].astype(F32) for i in range(3)]
    return terms[0] + terms[1] + terms[2]


def part_of(ref, index, strip, strips):
    start = (index * strips + strip) * SHARD
    return slice(start, start + SHARD)


def columns(strip):
    return slice(strip * 128, (strip + 1) * 128)


STEPS = (0, 1, -1, 2)


def place_text(at, core, parts, txt):
    x, y = at[0], at[1]
    for i, d in enumerate(STEPS):
        for j, e in enumerate(STEPS):
            dx, dy = jnp.where(core == 0, d, e), jnp.where(core == 0, e, d)
            txt[pl.ds(block_row(x - dx, y - dy), SHARD), :] = parts[i][j * SHARD : (j + 1) * SHARD, :]


def half_scores(scale, img, txt, scores, cols_out, row_top, row_sum):
    chunk = 512
    row_top[...] = jnp.full((ROWS, 128), -jnp.inf, F32)

    @pl.loop(0, PLANE // chunk)
    def _(i):
        cols = pl.ds(pl.multiple_of(i * chunk, chunk), chunk)
        s = scale * lax.dot_general(
            img[...], txt[cols, :], (((1,), (1,)), ((), ())), preferred_element_type=F32
        )
        scores[:, cols] = s
        tops = row_top[...]
        for j in range(chunk // 128):
            tops = jnp.maximum(tops, s[:, j * 128 : (j + 1) * 128])
        row_top[...] = tops
        top = jnp.max(s, axis=0, keepdims=True)
        cols_out[:, cols] = top + jnp.log(jnp.sum(jnp.exp(s - top), axis=0, keepdims=True))

    row_top[...] = jnp.broadcast_to(jnp.max(row_top[...], axis=1, keepdims=True), (ROWS, 128))
    row_sum[...] = jnp.zeros((ROWS, 128), F32)

    @pl.loop(0, PLANE // 256)
    def _(i):
        for j in range(2):
            cols = pl.ds(pl.multiple_of(i * 256 + j * 128, 128), 128)
            row_sum[...] += jnp.exp(scores[:, cols] - row_top[...])


def own_scores_kernel(scale, at, *refs):
    image_in, text_in = refs[:8], refs[8:12]
    img, txt, scores, cols_out, row_top, row_sum = refs[12:]
    for ref, step in zip(image_in, (0, -1, 1, -2, 2, -3, 3, -4)):
        where = lax.rem(at[2] + step + NZ, NZ) * SHARD
        img[pl.ds(pl.multiple_of(where, SHARD), SHARD), :] = ref[...]
    place_text(at, at[3], text_in, txt)
    half_scores(scale, img, txt, scores, cols_out, row_top, row_sum)


def other_scores_kernel(scale, at, *refs):
    text_in, (img, scores_own, cols_own, top_own, sum_own) = refs[:4], refs[4:9]
    txt, scores, row_out, col_out, cols_other, row_top, row_sum = refs[9:]
    x, y, z, c = at
    place_text(at, 1 - c, text_in, txt)
    half_scores(scale, img, txt, scores, cols_other, row_top, row_sum)
    top = jnp.maximum(row_top[...], top_own[...])
    total = row_sum[...] * jnp.exp(row_top[...] - top) + sum_own[...] * jnp.exp(top_own[...] - top)
    row = top + jnp.log(jnp.sum(total, axis=1, keepdims=True))
    row_out[...] = jnp.transpose(row)[0:1, :]
    col_out[:, pl.ds(pl.multiple_of(c * PLANE, PLANE), PLANE)] = cols_own[...]
    col_out[:, pl.ds(pl.multiple_of((1 - c) * PLANE, PLANE), PLANE)] = cols_other[...]
    col_out[:, COLS:] = jnp.zeros((1, 128), F32)

    @pl.when(has_diagonal(x, y, z))
    def _():
        mask = on_diagonal(x)
        total = jnp.zeros((1, 128), F32)
        for core, row, col in diagonal_blocks(c):
            rows, cols = slice(row, row + SHARD), pl.ds(col, 128)
            block = jnp.where(c == core, scores_own[rows, cols], scores[rows, cols])
            total += jnp.sum(jnp.where(mask, block, 0.0), axis=0, keepdims=True)
        col_out[:, COLS:] = jnp.broadcast_to(jnp.sum(total, axis=1, keepdims=True), (1, 128))


def line_kernel(text, *refs):
    near, line, sem = refs[:3], refs[3], refs[4]
    copy = pltpu.make_async_copy(text, line.at[pl.ds(0, SHARD)], sem)
    copy.start()
    for i, ref in enumerate(near, 1):
        line[i * SHARD : (i + 1) * SHARD, :] = ref[...]
    copy.wait()


def weights_kernel(at, scores_own, scores_other, row_lse, col_lse, own_out, other_out, p_out, q_out, row_col):
    x, y, z, c = at
    row_col[...] = jnp.transpose(jnp.broadcast_to(row_lse[...], (128, ROWS)))

    def weigh(s, rows, cols):
        return 0.5 * (jnp.exp(s - rows) + jnp.exp(s - cols))

    chunk = 128
    for half, scores, out in ((1 - c, scores_other, other_out), (c, scores_own, own_out)):

        @pl.loop(0, PLANE // chunk)
        def _(i, half=half, scores=scores, out=out):
            cols = pl.ds(pl.multiple_of(i * chunk, chunk), chunk)
            lse = col_lse[:, pl.ds(pl.multiple_of(half * PLANE + i * chunk, chunk), chunk)]
            out[:, cols] = weigh(scores[:, cols], row_col[...], lse).astype(BF16)

    @pl.when(has_diagonal(x, y, z))
    def _():
        mask = on_diagonal(x).astype(F32)
        for core, row, col in diagonal_blocks(c):

            def subtract(scores, out):
                rows, cols = pl.ds(row, SHARD), pl.ds(col, 128)
                lse = col_lse[:, pl.ds(pl.multiple_of(core * PLANE + col, 128), 128)]
                out[rows, cols] = (weigh(scores[rows, cols], row_col[rows, :], lse) - mask).astype(BF16)

            @pl.when(c == core)
            def _():
                subtract(scores_own, own_out)

            @pl.when(c != core)
            def _():
                subtract(scores_other, other_out)

    row_sum = 0.5 * jnp.sum(row_lse[...], axis=1, keepdims=True)
    p_out[...] = jnp.broadcast_to(row_sum, (1, 128))
    col_sum = 0.5 * jnp.sum(col_lse[:, :COLS], axis=1, keepdims=True)
    q_out[...] = jnp.broadcast_to(col_sum, (1, 128)) - col_lse[:, COLS:]


def image_kernel(steps, at, own, other, txt_own, txt_other, q, *refs):
    z, first_core = at[2], at[3] == 0
    far = refs[0] if steps[0][2] is None else None
    outs, (rows_own, rows_other, total) = refs[0 if far is None else 1 : -3], refs[-3:]
    for i, (dz, _, _) in enumerate(steps):
        rows = pl.ds(pl.multiple_of(lax.rem(z + dz + NZ, NZ) * SHARD, SHARD), SHARD)
        rows_own[i * SHARD : (i + 1) * SHARD, :] = own[rows, :]
        rows_other[i * SHARD : (i + 1) * SHARD, :] = other[rows, :]
    chunk = 256

    @pl.loop(0, total.shape[1] // chunk)
    def _(i):
        cols = pl.ds(pl.multiple_of(i * chunk, chunk), chunk)
        total[:, cols] = jnp.dot(rows_own[...], txt_own[:, cols], preferred_element_type=F32) + jnp.dot(
            rows_other[...], txt_other[:, cols], preferred_element_type=F32
        )

    strips = total.shape[1] // 128
    for i, (_, out, place) in enumerate(steps):
        for j in range(strips):
            block = total[i * SHARD : (i + 1) * SHARD, columns(j)]
            if place is None:
                if out:
                    far_rows = far[part_of(far, 0, j, strips), :].astype(F32)
                    block += jnp.where(first_core == (out == 1), far_rows, 0.0)
                outs[out][:, columns(j)] = block
            else:
                outs[out][part_of(outs[out], place, j, strips), :] = block.astype(BF16)
    for ref in outs:
        if ref.shape[1] == 128:
            write_note(ref, q[...])


def text_kernel(at, own, received, img, img_other, p_own, p_other, *refs):
    sent, kept, p_out, total = refs[:3], refs[3], refs[4], refs[5]
    x, y, _, c = at
    p = p_own[...] + p_other[...]
    p_out[...] = p
    chunk = 256

    @pl.loop(0, PLANE // chunk)
    def _(i):
        cols = pl.ds(pl.multiple_of(i * chunk, chunk), chunk)
        total[cols, :] = lax.dot_general(
            own[:, cols], img[...], (((0,), (0,)), ((), ())), preferred_element_type=F32
        ) + lax.dot_general(
            received[:, cols], img_other[...], (((0,), (0,)), ((), ())), preferred_element_type=F32
        )

    strips = total.shape[1] // 128
    for d in range(4):
        for e in range(4):
            dx, dy = jnp.where(c == 0, e, d), jnp.where(c == 0, d, e)
            rows = pl.ds(block_row(x + dx, y + dy), SHARD)
            for i in range(strips):
                part = total[rows, columns(i)]
                if d == 0:
                    kept[e * SHARD : (e + 1) * SHARD, columns(i)] = part
                else:
                    sent[d - 1][part_of(sent[d - 1], e, i, strips), :] = part.astype(BF16)
        if d:
            write_note(sent[d - 1], p)


def image_middle_kernel(at, up, down, far, here, up_two, down_two, q, up_out, down_out, here_out, q_out):
    first_core = at[3] == 0
    strips = here.shape[1] // 128
    for i in range(strips):
        near, rest, cols = part_of(up, 0, i, strips), part_of(up, 1, i, strips), columns(i)
        here_out[:, cols] = here[:, cols] + up[near, :].astype(F32) + down[near, :].astype(F32)
        above = up_two[:, cols] + up[rest, :].astype(F32)
        below = down_two[:, cols] + down[rest, :].astype(F32)
        up_out[near, :] = above.astype(BF16)
        down_out[near, :] = below.astype(BF16)
    note_up, note_down, note_far = read_note(up), read_note(down), read_note(far)
    write_note(up_out, q[...] + note_up + jnp.where(first_core, note_far, 0.0))
    write_note(down_out, q[...] + note_down + jnp.where(first_core, 0.0, note_far))
    q_out[...] = q[...] + note_up + note_down


def text_middle_kernel(at, first, second, third, kept, p, *refs):
    sent, kept_out, p_out = refs[:3], refs[3], refs[4]
    total = p[...] + read_note(first) + read_note(second) + read_note(third)
    p_out[...] = total
    strips = kept.shape[1] // 128
    for e in range(4):
        for i in range(strips):
            rows, cols = part_of(first, e, i, strips), columns(i)
            part = kept[e * SHARD : (e + 1) * SHARD, cols] + first[rows, :].astype(F32)
            part += second[rows, :].astype(F32) + third[rows, :].astype(F32)
            if e == 0:
                kept_out[:, cols] = part
            else:
                sent[e - 1][part_of(first, 0, i, strips), :] = part.astype(BF16)
        if e:
            write_note(sent[e - 1], total)


def last_kernel(at, up, down, here, q, first, second, third, kept, p, image_out, text_out, loss_out):
    strips = kept.shape[1] // 128
    for i in range(strips):
        rows, cols = part_of(up, 0, i, strips), columns(i)
        image = here[:, cols] + up[rows, :].astype(F32) + down[rows, :].astype(F32)
        image_out[:, cols] = image.astype(BF16)
        text = kept[:, cols] + first[rows, :].astype(F32) + second[rows, :].astype(F32) + third[rows, :].astype(F32)
        text_out[:, cols] = text.astype(BF16)
    loss = q[...] + p[...]
    for message in (up, down, first, second, third):
        loss += read_note(message)
    loss_out[...] = loss / (ROWS * NC * NX * NY)


def shards(image, text):
    embed = image.shape[1]
    scale = 4.0 / math.sqrt(embed)
    up, down = shift_z(image, 1), shift_z(image, -1)
    near = [shift_plane(text, d, True) for d in STEPS[1:]]
    line = pl.pallas_call(
        line_kernel,
        out_shape=jax.ShapeDtypeStruct((4 * SHARD, embed), BF16),
        in_specs=[pl.BlockSpec(memory_space=pltpu.HBM)] + [pl.BlockSpec(memory_space=pltpu.VMEM)] * 3,
        out_specs=pl.BlockSpec(memory_space=pltpu.VMEM),
        scratch_shapes=[pltpu.SemaphoreType.DMA],
        cost_estimate=pl.CostEstimate(flops=0, transcendentals=0, bytes_accessed=1 << 20),
        compiler_params=pltpu.CompilerParams(vmem_limit_bytes=4 << 20),
    )(text, *near)
    image_in = [image, up, down]
    up, down, line = lax.optimization_barrier((shift_z(up, 1), shift_z(down, -1), line))
    image_in += [up, down]
    far = [shift_plane(line, d, False) for d in STEPS[1:]]
    up, down = lax.optimization_barrier((shift_z(up, 1), shift_z(down, -1)))
    image_in += [up, down]
    last, line, *far = lax.optimization_barrier((shift_z(up, 1), line, *far))
    image_in.append(last)
    text_in = [line, *far]
    text_swapped = [swap_core(part) for part in text_in]

    tile = 2 * ROWS * COLS * embed
    half_scores_out = ((ROWS, PLANE), F32)
    lanes = ((ROWS, 128), F32)
    img, txt_own, scores_own, cols_own, top_own, sum_own = call(
        functools.partial(own_scores_kernel, scale),
        [((ROWS, embed), BF16), ((PLANE, embed), BF16), half_scores_out, ((1, PLANE), F32), lanes, lanes],
        image_in + text_in,
        [],
        tile // 2,
        ROWS * COLS,
        7 << 20,
        12,
    )
    txt_other, scores_other, row_lse, col_lse = call(
        functools.partial(other_scores_kernel, scale),
        [((PLANE, embed), BF16), half_scores_out, ((1, ROWS), F32), ((1, COLS + 128), F32)],
        [*text_swapped, img, scores_own, cols_own, top_own, sum_own],
        [pltpu.VMEM((1, PLANE), F32), pltpu.VMEM((ROWS, 128), F32), pltpu.VMEM((ROWS, 128), F32)],
        tile // 2,
        ROWS * COLS,
        7 << 20,
        14,
    )
    img_other = swap_core(img)
    col_lse = merge_columns(col_lse, swap_core(col_lse))
    for axis in (1, 0):
        col_lse = merge_columns(col_lse, *[shift_one(col_lse, axis, by) for by in STEPS[1:]])
    for bit in (1, 2, 4):
        row_lse = merge(row_lse, swap(row_lse, 2, bit))

    half = ((ROWS, PLANE), BF16)
    scalar = ((1, 128), F32)
    own, other, p, q = call(
        weights_kernel,
        [half, half, scalar, scalar],
        (scores_own, scores_other, row_lse, col_lse),
        [pltpu.VMEM((ROWS, 128), F32)],
        8 * ROWS * COLS,
        2 * ROWS * COLS,
        6 << 20,
        12,
    )
    received = swap_core(other)
    p_other = swap_core(p)
    message = lambda rows: ((rows * embed // 128 + NOTE, 128), BF16)
    image_part = lambda steps, outs, other, *far: call(
        functools.partial(image_kernel, steps),
        outs,
        (own, other, txt_own, txt_other, q, *far),
        [pltpu.VMEM((len(steps) * SHARD, PLANE), BF16)] * 2 + [pltpu.VMEM((len(steps) * SHARD, embed), F32)],
        tile // 2,
        0,
        8 << 20,
        16,
    )
    up, down, far = image_part(
        ((1, 0, 0), (3, 0, 1), (-1, 1, 0), (-3, 1, 1), (4, 2, 0)), [message(2 * SHARD)] * 2 + [message(SHARD)], other
    )
    received, up = lax.optimization_barrier((received, up))
    far = shift_far(far)
    *sent, kept, p = call(
        text_kernel,
        [message(4 * SHARD)] * 3 + [((4 * SHARD, embed), F32), scalar],
        (own, received, img, img_other, p, p_other),
        [pltpu.VMEM((PLANE, embed), F32)],
        tile // 2,
        0,
        12 << 20,
        24,
    )
    other, kept = lax.optimization_barrier((other, kept))
    here, up_two, down_two = image_part(
        ((0, 0, None), (2, 1, None), (-2, 2, None)), [((SHARD, embed), F32)] * 3, other, far
    )
    up, down = shift_z(up, 1), shift_z(down, -1)
    sent = [shift_plane(part, d, True) for d, part in enumerate(sent, 1)]
    up, down, here, q = call(
        image_middle_kernel,
        [message(SHARD)] * 2 + [((SHARD, embed), F32), scalar],
        (up, down, far, here, up_two, down_two, q),
        [],
        1 << 20,
        0,
        2 << 20,
        12,
    )
    up, down = shift_z(up, 2), shift_z(down, -2)
    *sent, kept, p = call(
        text_middle_kernel,
        [message(SHARD)] * 3 + [((SHARD, embed), F32), scalar],
        (*sent, kept, p),
        [],
        1 << 20,
        0,
        4 << 20,
        12,
    )
    sent = [shift_plane(part, d, False) for d, part in enumerate(sent, 1)]
    image_grad, text_grad, loss = call(
        last_kernel,
        [((SHARD, embed), BF16)] * 2 + [scalar],
        (up, down, here, q, *sent, kept, p),
        [],
        1 << 20,
        0,
        2 << 20,
        12,
    )
    return image_grad, text_grad, loss[0, 0]


def solution(mesh):
    return jax.shard_map(
        shards,
        mesh=mesh,
        in_specs=(P(("img", "txt"), None), P(("txt", "img"), None)),
        out_specs=(P(("img", "txt"), None), P(("txt", "img"), None), P()),
        check_vma=False,
    )
```

```python
import functools
import math

import jax
import jax.numpy as jnp
from jax import lax
from jax.experimental import pallas as pl
from jax.experimental.pallas import tpu as pltpu
from jax.sharding import PartitionSpec as P

NX, NY, NZ, NC = 4, 4, 8, 2
AXES = ("img", "txt")
SHARD = 64
HALF = SHARD // 2
ROWS = NZ * SHARD
PLANE = NX * NY * SHARD
COLS = NC * PLANE
NOTE = 16
BF16, F32 = jnp.bfloat16, jnp.float32


def device_id(x, y, z, c):
    return (((x % NX) * NY + y % NY) * NZ + z % NZ) * NC + c % NC


COORDINATES = [(x, y, z, c) for x in range(NX) for y in range(NY) for z in range(NZ) for c in range(NC)]


def shift_z(value, by):
    pairs = [(device_id(x, y, z, c), device_id(x, y, z + by, c)) for x, y, z, c in COORDINATES]
    return lax.ppermute(value, AXES, pairs)


def shift_plane(value, by, first):
    pairs = []
    for x, y, z, c in COORDINATES:
        along_y = (c == 0) == first
        to = (x, y + by) if along_y else (x + by, y)
        pairs.append((device_id(x, y, z, c), device_id(*to, z, c)))
    return lax.ppermute(value, AXES, pairs)


def shift_far(value):
    pairs = [(device_id(x, y, z, c), device_id(x, y, z + 2 - 4 * c, c)) for x, y, z, c in COORDINATES]
    return lax.ppermute(value, AXES, pairs)


def swap(value, axis, bit):
    pairs = []
    for at in COORDINATES:
        to = list(at)
        to[axis] ^= bit
        pairs.append((device_id(*at), device_id(*to)))
    return lax.ppermute(value, AXES, pairs)


def swap_core(value):
    return swap(value, 3, 1)


def merge(*parts):
    top = functools.reduce(jnp.maximum, parts)
    return top + jnp.log(sum(jnp.exp(part - top) for part in parts))


def merge_columns(*parts):
    lanes = lax.broadcasted_iota(jnp.int32, parts[0].shape, 1)
    return jnp.where(lanes < COLS, merge(*parts), sum(parts))


def shift_one(value, axis, by):
    pairs = []
    for at in COORDINATES:
        to = list(at)
        to[axis] += by
        pairs.append((device_id(*at), device_id(*to)))
    return lax.ppermute(value, AXES, pairs)


def position():
    img, txt = lax.axis_index("img"), lax.axis_index("txt")
    y = lax.rem(img, 2) * 2 + txt // (NZ * NC)
    return img // 2, y, lax.rem(txt // NC, NZ), lax.rem(txt, NC)


def call(kernel, outs, args, scratch, flops, transcendentals, moved, vmem_mib):
    vmem = pl.BlockSpec(memory_space=pltpu.VMEM)
    return pl.pallas_call(
        lambda *refs: kernel(position(), *refs),
        out_shape=[jax.ShapeDtypeStruct(shape, dtype) for shape, dtype in outs],
        in_specs=[vmem] * len(args),
        out_specs=[vmem] * len(outs),
        scratch_shapes=scratch,
        cost_estimate=pl.CostEstimate(flops=8 * flops, transcendentals=transcendentals, bytes_accessed=moved),
        compiler_params=pltpu.CompilerParams(vmem_limit_bytes=vmem_mib << 20),
    )(*args)


def diagonal_blocks(c):
    for zz in range(NZ):
        yield zz // 4, zz * SHARD, pl.multiple_of((zz % 4) * NY * SHARD + c * 2 * SHARD, 128)


def on_diagonal(x):
    rows = lax.broadcasted_iota(jnp.int32, (SHARD, 128), 0)
    lanes = lax.broadcasted_iota(jnp.int32, (SHARD, 128), 1)
    return lanes == rows + (x // 2) * SHARD


def has_diagonal(x, y, z):
    return z == (x % 2) * 4 + y


def block_row(xx, yy):
    return pl.multiple_of((lax.rem(xx + NX, NX) * NY + lax.rem(yy + NY, NY)) * SHARD, SHARD)


def write_note(ref, value):
    high = value.astype(BF16).astype(F32)
    middle = (value - high).astype(BF16).astype(F32)
    low = value - high - middle
    which = lax.broadcasted_iota(jnp.int32, (NOTE, 128), 0)
    rows = jnp.where(which == 0, high, jnp.where(which == 1, middle, jnp.where(which == 2, low, 0.0)))
    ref[ref.shape[0] - NOTE :, :] = rows.astype(BF16)


def read_note(ref):
    terms = [ref[ref.shape[0] - NOTE + i : ref.shape[0] - NOTE + i + 1, :].astype(F32) for i in range(3)]
    return terms[0] + terms[1] + terms[2]


def part_of(ref, index, strip, strips):
    start = (index * strips + strip) * SHARD
    return slice(start, start + SHARD)


def columns(strip):
    return slice(strip * 128, (strip + 1) * 128)


STEPS = (0, 1, -1, 2)


def place_text(at, core, parts, txt):
    x, y = at[0], at[1]
    for i, d in enumerate(STEPS):
        for j, e in enumerate(STEPS):
            dx, dy = jnp.where(core == 0, d, e), jnp.where(core == 0, e, d)
            txt[pl.ds(block_row(x - dx, y - dy), SHARD), :] = parts[i][j * SHARD : (j + 1) * SHARD, :]


def half_scores(scale, img, txt, scores, cols_out, row_top, row_sum):
    chunk = 512
    row_top[...] = jnp.full((ROWS, 128), -jnp.inf, F32)
    row_sum[...] = jnp.zeros((ROWS, 128), F32)

    def multiply(i):
        cols = slice(i * chunk, (i + 1) * chunk)
        scores[:, cols] = scale * lax.dot_general(
            img[...], txt[cols, :], (((1,), (1,)), ((), ())), preferred_element_type=F32
        )

    def reduce(i):
        cols = slice(i * chunk, (i + 1) * chunk)
        s = scores[:, cols]
        lanes = [s[:, j * 128 : (j + 1) * 128] for j in range(chunk // 128)]
        before = row_top[...]
        tops = functools.reduce(jnp.maximum, lanes, before)
        row_top[...] = tops
        row_sum[...] = row_sum[...] * jnp.exp(before - tops) + sum(jnp.exp(part - tops) for part in lanes)
        top = jnp.max(s, axis=0, keepdims=True)
        cols_out[:, cols] = top + jnp.log(jnp.sum(jnp.exp(s - top), axis=0, keepdims=True))

    multiply(0)
    for i in range(1, PLANE // chunk):
        reduce(i - 1)
        multiply(i)
    reduce(PLANE // chunk - 1)


def own_scores_kernel(scale, at, *refs):
    image_in, text_in = refs[:8], refs[8:12]
    img, txt, scores, cols_out, row_top, row_sum = refs[12:]
    for ref, step in zip(image_in, (0, -1, 1, -2, 2, -3, 3, -4)):
        where = lax.rem(at[2] + step + NZ, NZ) * SHARD
        img[pl.ds(pl.multiple_of(where, SHARD), SHARD), :] = ref[...]
    place_text(at, at[3], text_in, txt)
    half_scores(scale, img, txt, scores, cols_out, row_top, row_sum)


def other_scores_kernel(scale, at, *refs):
    text_in, (img, scores_own, cols_own, top_own, sum_own) = refs[:4], refs[4:9]
    txt, scores, row_out, col_out, cols_other, row_top, row_sum = refs[9:]
    x, y, z, c = at
    place_text(at, 1 - c, text_in, txt)
    half_scores(scale, img, txt, scores, cols_other, row_top, row_sum)
    top = jnp.max(jnp.maximum(row_top[...], top_own[...]), axis=1, keepdims=True)
    total = row_sum[...] * jnp.exp(row_top[...] - top) + sum_own[...] * jnp.exp(top_own[...] - top)
    row = top + jnp.log(jnp.sum(total, axis=1, keepdims=True))
    row_out[...] = jnp.transpose(jnp.broadcast_to(row, (ROWS, 128)))[0:1, :]
    col_out[:, pl.ds(pl.multiple_of(c * PLANE, PLANE), PLANE)] = cols_own[...]
    col_out[:, pl.ds(pl.multiple_of((1 - c) * PLANE, PLANE), PLANE)] = cols_other[...]
    col_out[:, COLS:] = jnp.zeros((1, 128), F32)

    @pl.when(has_diagonal(x, y, z))
    def _():
        mask = on_diagonal(x)
        total = jnp.zeros((1, 128), F32)
        for core, row, col in diagonal_blocks(c):
            rows, cols = slice(row, row + SHARD), pl.ds(col, 128)
            block = jnp.where(c == core, scores_own[rows, cols], scores[rows, cols])
            total += jnp.sum(jnp.where(mask, block, 0.0), axis=0, keepdims=True)
        col_out[:, COLS:] = jnp.broadcast_to(jnp.sum(total, axis=1, keepdims=True), (1, 128))


def line_kernel(text, *refs):
    near, line, sem = refs[:3], refs[3], refs[4]
    copy = pltpu.make_async_copy(text, line.at[pl.ds(0, SHARD)], sem)
    copy.start()
    for i, ref in enumerate(near, 1):
        line[i * SHARD : (i + 1) * SHARD, :] = ref[...]
    copy.wait()


def weights_kernel(at, scores_own, scores_other, row_lse, col_lse, own_out, other_out, p_out, q_out, row_col):
    x, y, z, c = at
    row_col[...] = jnp.transpose(jnp.broadcast_to(row_lse[...], (128, ROWS)))

    def weigh(s, rows, cols):
        return 0.5 * (jnp.exp(s - rows) + jnp.exp(s - cols))

    chunk = 128
    for half, scores, out in ((1 - c, scores_other, other_out), (c, scores_own, own_out)):

        @pl.loop(0, PLANE // chunk)
        def _(i, half=half, scores=scores, out=out):
            cols = pl.ds(pl.multiple_of(i * chunk, chunk), chunk)
            lse = col_lse[:, pl.ds(pl.multiple_of(half * PLANE + i * chunk, chunk), chunk)]
            out[:, cols] = weigh(scores[:, cols], row_col[...], lse).astype(BF16)

    @pl.when(has_diagonal(x, y, z))
    def _():
        mask = on_diagonal(x).astype(F32)
        for core, row, col in diagonal_blocks(c):

            def subtract(scores, out):
                rows, cols = pl.ds(row, SHARD), pl.ds(col, 128)
                lse = col_lse[:, pl.ds(pl.multiple_of(core * PLANE + col, 128), 128)]
                out[rows, cols] = (weigh(scores[rows, cols], row_col[rows, :], lse) - mask).astype(BF16)

            @pl.when(c == core)
            def _():
                subtract(scores_own, own_out)

            @pl.when(c != core)
            def _():
                subtract(scores_other, other_out)

    row_sum = 0.5 * jnp.sum(row_lse[...], axis=1, keepdims=True)
    p_out[...] = jnp.broadcast_to(row_sum, (1, 128))
    col_sum = 0.5 * jnp.sum(col_lse[:, :COLS], axis=1, keepdims=True)
    q_out[...] = jnp.broadcast_to(col_sum, (1, 128)) - col_lse[:, COLS:]


def image_kernel(steps, at, own, other, txt_own, txt_other, q, *refs):
    z, first_core = at[2], at[3] == 0
    far = refs[0] if steps[0][2] is None else None
    outs, (rows_own, rows_other, total) = refs[0 if far is None else 1 : -3], refs[-3:]
    for i, (dz, _, _) in enumerate(steps):
        rows = pl.ds(pl.multiple_of(lax.rem(z + dz + NZ, NZ) * SHARD, SHARD), SHARD)
        rows_own[i * SHARD : (i + 1) * SHARD, :] = own[rows, :]
        rows_other[i * SHARD : (i + 1) * SHARD, :] = other[rows, :]
    chunk = 256

    @pl.loop(0, total.shape[1] // chunk)
    def _(i):
        cols = pl.ds(pl.multiple_of(i * chunk, chunk), chunk)
        total[:, cols] = jnp.dot(rows_own[...], txt_own[:, cols], preferred_element_type=F32) + jnp.dot(
            rows_other[...], txt_other[:, cols], preferred_element_type=F32
        )

    strips = total.shape[1] // 128
    for i, (_, out, place) in enumerate(steps):
        for j in range(strips):
            block = total[i * SHARD : (i + 1) * SHARD, columns(j)]
            if place is None:
                if out:
                    far_rows = far[part_of(far, 0, j, strips), :].astype(F32)
                    block += jnp.where(first_core == (out == 1), far_rows, 0.0)
                outs[out][:, columns(j)] = block
            else:
                outs[out][part_of(outs[out], place, j, strips), :] = block.astype(BF16)
    for ref in outs:
        if ref.shape[1] == 128:
            write_note(ref, q[...])


def text_kernel(at, own, received, img, img_other, p_own, p_other, *refs):
    sent, kept, p_out, total = refs[:3], refs[3], refs[4], refs[5]
    x, y, _, c = at
    p = p_own[...] + p_other[...]
    p_out[...] = p
    chunk = 256

    @pl.loop(0, PLANE // chunk)
    def _(i):
        cols = pl.ds(pl.multiple_of(i * chunk, chunk), chunk)
        total[cols, :] = lax.dot_general(
            own[:, cols], img[...], (((0,), (0,)), ((), ())), preferred_element_type=F32
        ) + lax.dot_general(
            received[:, cols], img_other[...], (((0,), (0,)), ((), ())), preferred_element_type=F32
        )

    strips = total.shape[1] // 128
    for d in range(4):
        for e in range(4):
            dx, dy = jnp.where(c == 0, e, d), jnp.where(c == 0, d, e)
            rows = pl.ds(block_row(x + dx, y + dy), SHARD)
            for i in range(strips):
                part = total[rows, columns(i)]
                if d == 0:
                    kept[e * SHARD : (e + 1) * SHARD, columns(i)] = part
                else:
                    sent[d - 1][part_of(sent[d - 1], e, i, strips), :] = part.astype(BF16)
        if d:
            write_note(sent[d - 1], p)


def image_middle_kernel(at, up, down, far, here, up_two, down_two, q, up_out, down_out, here_out, q_out):
    first_core = at[3] == 0
    strips = here.shape[1] // 128
    for i in range(strips):
        near, rest, cols = part_of(up, 0, i, strips), part_of(up, 1, i, strips), columns(i)
        here_out[:, cols] = here[:, cols] + up[near, :].astype(F32) + down[near, :].astype(F32)
        above = up_two[:, cols] + up[rest, :].astype(F32)
        below = down_two[:, cols] + down[rest, :].astype(F32)
        up_out[near, :] = above.astype(BF16)
        down_out[near, :] = below.astype(BF16)
    note_up, note_down, note_far = read_note(up), read_note(down), read_note(far)
    write_note(up_out, q[...] + note_up + jnp.where(first_core, note_far, 0.0))
    write_note(down_out, q[...] + note_down + jnp.where(first_core, 0.0, note_far))
    q_out[...] = q[...] + note_up + note_down


def text_middle_kernel(at, first, second, third, kept, p, *refs):
    sent, kept_out, p_out = refs[:3], refs[3], refs[4]
    total = p[...] + read_note(first) + read_note(second) + read_note(third)
    p_out[...] = total
    strips = kept.shape[1] // 128
    for e in range(4):
        for i in range(strips):
            rows, cols = part_of(first, e, i, strips), columns(i)
            part = kept[e * SHARD : (e + 1) * SHARD, cols] + first[rows, :].astype(F32)
            part += second[rows, :].astype(F32) + third[rows, :].astype(F32)
            if e == 0:
                kept_out[:, cols] = part
            else:
                sent[e - 1][part_of(first, 0, i, strips), :] = part.astype(BF16)
        if e:
            write_note(sent[e - 1], total)


def last_kernel(at, up, down, here, q, first, second, third, kept, p, image_out, text_out, loss_out):
    strips = kept.shape[1] // 128
    for i in range(strips):
        rows, cols = part_of(up, 0, i, strips), columns(i)
        image = here[:, cols] + up[rows, :].astype(F32) + down[rows, :].astype(F32)
        image_out[:, cols] = image.astype(BF16)
        text = kept[:, cols] + first[rows, :].astype(F32) + second[rows, :].astype(F32) + third[rows, :].astype(F32)
        text_out[:, cols] = text.astype(BF16)
    loss = q[...] + p[...]
    for message in (up, down, first, second, third):
        loss += read_note(message)
    loss_out[...] = loss / (ROWS * NC * NX * NY)


def shards(image, text):
    embed = image.shape[1]
    scale = 4.0 / math.sqrt(embed)
    up, down = shift_z(image, 1), shift_z(image, -1)
    near = [shift_plane(text, d, True) for d in STEPS[1:]]
    line = pl.pallas_call(
        line_kernel,
        out_shape=jax.ShapeDtypeStruct((4 * SHARD, embed), BF16),
        in_specs=[pl.BlockSpec(memory_space=pltpu.HBM)] + [pl.BlockSpec(memory_space=pltpu.VMEM)] * 3,
        out_specs=pl.BlockSpec(memory_space=pltpu.VMEM),
        scratch_shapes=[pltpu.SemaphoreType.DMA],
        cost_estimate=pl.CostEstimate(flops=0, transcendentals=0, bytes_accessed=1 << 20),
        compiler_params=pltpu.CompilerParams(vmem_limit_bytes=4 << 20),
    )(text, *near)
    image_in = [image, up, down]
    up, down, line = lax.optimization_barrier((shift_z(up, 1), shift_z(down, -1), line))
    image_in += [up, down]
    far = [shift_plane(line, d, False) for d in STEPS[1:]]
    up, down = lax.optimization_barrier((shift_z(up, 1), shift_z(down, -1)))
    image_in += [up, down]
    line_sent, up = lax.optimization_barrier((line, up))
    last, *far = lax.optimization_barrier((shift_z(up, 1), *far))
    image_in.append(last)
    text_in = [line, *far]
    text_swapped = [swap_core(part) for part in (line_sent, *far)]

    tile = 2 * ROWS * COLS * embed
    half_scores_out = ((ROWS, PLANE), F32)
    lanes = ((ROWS, 128), F32)
    img, txt_own, scores_own, cols_own, top_own, sum_own = call(
        functools.partial(own_scores_kernel, scale),
        [((ROWS, embed), BF16), ((PLANE, embed), BF16), half_scores_out, ((1, PLANE), F32), lanes, lanes],
        image_in + text_in,
        [],
        tile // 2,
        ROWS * COLS,
        7 << 20,
        12,
    )
    txt_other, scores_other, row_lse, col_lse = call(
        functools.partial(other_scores_kernel, scale),
        [((PLANE, embed), BF16), half_scores_out, ((1, ROWS), F32), ((1, COLS + 128), F32)],
        [*text_swapped, img, scores_own, cols_own, top_own, sum_own],
        [pltpu.VMEM((1, PLANE), F32), pltpu.VMEM((ROWS, 128), F32), pltpu.VMEM((ROWS, 128), F32)],
        tile // 2,
        ROWS * COLS,
        7 << 20,
        14,
    )
    img_other = swap_core(img)
    col_lse = merge_columns(col_lse, swap_core(col_lse))
    for axis in (1, 0):
        col_lse = merge_columns(col_lse, *[shift_one(col_lse, axis, by) for by in STEPS[1:]])
    for bit in (1, 2, 4):
        row_lse = merge(row_lse, swap(row_lse, 2, bit))

    half = ((ROWS, PLANE), BF16)
    scalar = ((1, 128), F32)
    own, other, p, q = call(
        weights_kernel,
        [half, half, scalar, scalar],
        (scores_own, scores_other, row_lse, col_lse),
        [pltpu.VMEM((ROWS, 128), F32)],
        8 * ROWS * COLS,
        2 * ROWS * COLS,
        6 << 20,
        12,
    )
    received = swap_core(other)
    p_other = swap_core(p)
    message = lambda rows: ((rows * embed // 128 + NOTE, 128), BF16)
    image_part = lambda steps, outs, other, *far: call(
        functools.partial(image_kernel, steps),
        outs,
        (own, other, txt_own, txt_other, q, *far),
        [pltpu.VMEM((len(steps) * SHARD, PLANE), BF16)] * 2 + [pltpu.VMEM((len(steps) * SHARD, embed), F32)],
        tile // 2,
        0,
        8 << 20,
        16,
    )
    up, down, far = image_part(
        ((1, 0, 0), (3, 0, 1), (-1, 1, 0), (-3, 1, 1), (4, 2, 0)), [message(2 * SHARD)] * 2 + [message(SHARD)], other
    )
    received, up = lax.optimization_barrier((received, up))
    far = shift_far(far)
    *sent, kept, p = call(
        text_kernel,
        [message(4 * SHARD)] * 3 + [((4 * SHARD, embed), F32), scalar],
        (own, received, img, img_other, p, p_other),
        [pltpu.VMEM((PLANE, embed), F32)],
        tile // 2,
        0,
        12 << 20,
        24,
    )
    other, kept = lax.optimization_barrier((other, kept))
    here, up_two, down_two = image_part(
        ((0, 0, None), (2, 1, None), (-2, 2, None)), [((SHARD, embed), F32)] * 3, other, far
    )
    up, down, here = lax.optimization_barrier((up, down, here))
    up, down = shift_z(up, 1), shift_z(down, -1)
    sent = [shift_plane(part, d, True) for d, part in enumerate(sent, 1)]
    up, down, here, q = call(
        image_middle_kernel,
        [message(SHARD)] * 2 + [((SHARD, embed), F32), scalar],
        (up, down, far, here, up_two, down_two, q),
        [],
        1 << 20,
        0,
        2 << 20,
        12,
    )
    up, down = shift_z(up, 2), shift_z(down, -2)
    *sent, kept, p = call(
        text_middle_kernel,
        [message(SHARD)] * 3 + [((SHARD, embed), F32), scalar],
        (*sent, kept, p),
        [],
        1 << 20,
        0,
        4 << 20,
        12,
    )
    sent = [shift_plane(part, d, False) for d, part in enumerate(sent, 1)]
    image_grad, text_grad, loss = call(
        last_kernel,
        [((SHARD, embed), BF16)] * 2 + [scalar],
        (up, down, here, q, *sent, kept, p),
        [],
        1 << 20,
        0,
        2 << 20,
        12,
    )
    return image_grad, text_grad, loss[0, 0]


def solution(mesh):
    return jax.shard_map(
        shards,
        mesh=mesh,
        in_specs=(P(("img", "txt"), None), P(("txt", "img"), None)),
        out_specs=(P(("img", "txt"), None), P(("txt", "img"), None), P()),
        check_vma=False,
    )
```

```python
import functools
import math

import jax
import jax.numpy as jnp
from jax import lax
from jax.experimental import pallas as pl
from jax.experimental.pallas import tpu as pltpu
from jax.sharding import PartitionSpec as P

NX, NY, NZ, NC = 4, 4, 8, 2
AXES = ("img", "txt")
SHARD = 64
HALF = SHARD // 2
ROWS = NZ * SHARD
PLANE = NX * NY * SHARD
COLS = NC * PLANE
NOTE = 16
BF16, F32 = jnp.bfloat16, jnp.float32


def device_id(x, y, z, c):
    return (((x % NX) * NY + y % NY) * NZ + z % NZ) * NC + c % NC


COORDINATES = [(x, y, z, c) for x in range(NX) for y in range(NY) for z in range(NZ) for c in range(NC)]


def shift_z(value, by):
    pairs = [(device_id(x, y, z, c), device_id(x, y, z + by, c)) for x, y, z, c in COORDINATES]
    return lax.ppermute(value, AXES, pairs)


def shift_plane(value, by, first):
    pairs = []
    for x, y, z, c in COORDINATES:
        along_y = (c == 0) == first
        to = (x, y + by) if along_y else (x + by, y)
        pairs.append((device_id(x, y, z, c), device_id(*to, z, c)))
    return lax.ppermute(value, AXES, pairs)


def shift_far(value):
    pairs = [(device_id(x, y, z, c), device_id(x, y, z + 2 - 4 * c, c)) for x, y, z, c in COORDINATES]
    return lax.ppermute(value, AXES, pairs)


def swap(value, axis, bit):
    pairs = []
    for at in COORDINATES:
        to = list(at)
        to[axis] ^= bit
        pairs.append((device_id(*at), device_id(*to)))
    return lax.ppermute(value, AXES, pairs)


def swap_core(value):
    return swap(value, 3, 1)


def merge(*parts):
    top = functools.reduce(jnp.maximum, parts)
    return top + jnp.log(sum(jnp.exp(part - top) for part in parts))


def merge_columns(*parts):
    lanes = lax.broadcasted_iota(jnp.int32, parts[0].shape, 1)
    return jnp.where(lanes < COLS, merge(*parts), sum(parts))


def shift_one(value, axis, by):
    pairs = []
    for at in COORDINATES:
        to = list(at)
        to[axis] += by
        pairs.append((device_id(*at), device_id(*to)))
    return lax.ppermute(value, AXES, pairs)


def position():
    img, txt = lax.axis_index("img"), lax.axis_index("txt")
    y = lax.rem(img, 2) * 2 + txt // (NZ * NC)
    return img // 2, y, lax.rem(txt // NC, NZ), lax.rem(txt, NC)


def call(kernel, outs, args, scratch, flops, transcendentals, moved, vmem_mib):
    vmem = pl.BlockSpec(memory_space=pltpu.VMEM)
    return pl.pallas_call(
        lambda *refs: kernel(position(), *refs),
        out_shape=[jax.ShapeDtypeStruct(shape, dtype) for shape, dtype in outs],
        in_specs=[vmem] * len(args),
        out_specs=[vmem] * len(outs),
        scratch_shapes=scratch,
        cost_estimate=pl.CostEstimate(flops=8 * flops, transcendentals=transcendentals, bytes_accessed=moved),
        compiler_params=pltpu.CompilerParams(vmem_limit_bytes=vmem_mib << 20),
    )(*args)


def diagonal_blocks(c):
    for zz in range(NZ):
        yield zz // 4, zz * SHARD, pl.multiple_of((zz % 4) * NY * SHARD + c * 2 * SHARD, 128)


def on_diagonal(x):
    rows = lax.broadcasted_iota(jnp.int32, (SHARD, 128), 0)
    lanes = lax.broadcasted_iota(jnp.int32, (SHARD, 128), 1)
    return lanes == rows + (x // 2) * SHARD


def has_diagonal(x, y, z):
    return z == (x % 2) * 4 + y


def block_row(xx, yy):
    return pl.multiple_of((lax.rem(xx + NX, NX) * NY + lax.rem(yy + NY, NY)) * SHARD, SHARD)


def write_note(ref, value):
    high = value.astype(BF16).astype(F32)
    middle = (value - high).astype(BF16).astype(F32)
    low = value - high - middle
    which = lax.broadcasted_iota(jnp.int32, (NOTE, 128), 0)
    rows = jnp.where(which == 0, high, jnp.where(which == 1, middle, jnp.where(which == 2, low, 0.0)))
    ref[ref.shape[0] - NOTE :, :] = rows.astype(BF16)


def read_note(ref):
    terms = [ref[ref.shape[0] - NOTE + i : ref.shape[0] - NOTE + i + 1, :].astype(F32) for i in range(3)]
    return terms[0] + terms[1] + terms[2]


def part_of(ref, index, strip, strips):
    start = (index * strips + strip) * SHARD
    return slice(start, start + SHARD)


def columns(strip):
    return slice(strip * 128, (strip + 1) * 128)


STEPS = (0, 1, -1, 2)


def place_text(at, core, parts, txt):
    x, y = at[0], at[1]
    for i, d in enumerate(STEPS):
        for j, e in enumerate(STEPS):
            dx, dy = jnp.where(core == 0, d, e), jnp.where(core == 0, e, d)
            txt[pl.ds(block_row(x - dx, y - dy), SHARD), :] = parts[i][j * SHARD : (j + 1) * SHARD, :]


def half_scores(scale, img, txt, scores, cols_out, row_top, row_sum):
    chunk = 512
    row_top[...] = jnp.full((ROWS, 128), -jnp.inf, F32)
    row_sum[...] = jnp.zeros((ROWS, 128), F32)

    def multiply(i):
        cols = slice(i * chunk, (i + 1) * chunk)
        scores[:, cols] = scale * lax.dot_general(
            img[...], txt[cols, :], (((1,), (1,)), ((), ())), preferred_element_type=F32
        )

    def reduce(i):
        cols = slice(i * chunk, (i + 1) * chunk)
        s = scores[:, cols]
        lanes = [s[:, j * 128 : (j + 1) * 128] for j in range(chunk // 128)]
        before = row_top[...]
        tops = functools.reduce(jnp.maximum, lanes, before)
        row_top[...] = tops
        row_sum[...] = row_sum[...] * jnp.exp(before - tops) + sum(jnp.exp(part - tops) for part in lanes)
        top = jnp.max(s, axis=0, keepdims=True)
        cols_out[:, cols] = top + jnp.log(jnp.sum(jnp.exp(s - top), axis=0, keepdims=True))

    multiply(0)
    for i in range(1, PLANE // chunk):
        reduce(i - 1)
        multiply(i)
    reduce(PLANE // chunk - 1)


def own_scores_kernel(scale, at, *refs):
    image_in, text_in = refs[:8], refs[8:12]
    img, txt, scores, cols_out, row_top, row_sum = refs[12:]
    for ref, step in zip(image_in, (0, -1, 1, -2, 2, -3, 3, -4)):
        where = lax.rem(at[2] + step + NZ, NZ) * SHARD
        img[pl.ds(pl.multiple_of(where, SHARD), SHARD), :] = ref[...]
    place_text(at, at[3], text_in, txt)
    half_scores(scale, img, txt, scores, cols_out, row_top, row_sum)


def other_scores_kernel(scale, at, *refs):
    text_in, (img, scores_own, cols_own, top_own, sum_own) = refs[:4], refs[4:9]
    txt, scores, row_out, col_out, cols_other, row_top, row_sum = refs[9:]
    x, y, z, c = at
    place_text(at, 1 - c, text_in, txt)
    half_scores(scale, img, txt, scores, cols_other, row_top, row_sum)
    top = jnp.max(jnp.maximum(row_top[...], top_own[...]), axis=1, keepdims=True)
    total = row_sum[...] * jnp.exp(row_top[...] - top) + sum_own[...] * jnp.exp(top_own[...] - top)
    row = top + jnp.log(jnp.sum(total, axis=1, keepdims=True))
    row_out[...] = jnp.transpose(jnp.broadcast_to(row, (ROWS, 128)))[0:1, :]
    col_out[:, pl.ds(pl.multiple_of(c * PLANE, PLANE), PLANE)] = cols_own[...]
    col_out[:, pl.ds(pl.multiple_of((1 - c) * PLANE, PLANE), PLANE)] = cols_other[...]
    col_out[:, COLS:] = jnp.zeros((1, 128), F32)

    @pl.when(has_diagonal(x, y, z))
    def _():
        mask = on_diagonal(x)
        total = jnp.zeros((1, 128), F32)
        for core, row, col in diagonal_blocks(c):
            rows, cols = slice(row, row + SHARD), pl.ds(col, 128)
            block = jnp.where(c == core, scores_own[rows, cols], scores[rows, cols])
            total += jnp.sum(jnp.where(mask, block, 0.0), axis=0, keepdims=True)
        col_out[:, COLS:] = jnp.broadcast_to(jnp.sum(total, axis=1, keepdims=True), (1, 128))


def line_kernel(text, *refs):
    near, line, sem = refs[:3], refs[3], refs[4]
    copy = pltpu.make_async_copy(text, line.at[pl.ds(0, SHARD)], sem)
    copy.start()
    for i, ref in enumerate(near, 1):
        line[i * SHARD : (i + 1) * SHARD, :] = ref[...]
    copy.wait()


def weights_kernel(at, scores_own, scores_other, row_lse, col_lse, own_out, other_out, p_out, q_out, row_col):
    x, y, z, c = at
    row_col[...] = jnp.transpose(jnp.broadcast_to(row_lse[...], (128, ROWS)))

    def weigh(s, rows, cols):
        return 0.5 * (jnp.exp(s - rows) + jnp.exp(s - cols))

    chunk = 128
    for half, scores, out in ((1 - c, scores_other, other_out), (c, scores_own, own_out)):

        @pl.loop(0, PLANE // chunk)
        def _(i, half=half, scores=scores, out=out):
            cols = pl.ds(pl.multiple_of(i * chunk, chunk), chunk)
            lse = col_lse[:, pl.ds(pl.multiple_of(half * PLANE + i * chunk, chunk), chunk)]
            out[:, cols] = weigh(scores[:, cols], row_col[...], lse).astype(BF16)

    @pl.when(has_diagonal(x, y, z))
    def _():
        mask = on_diagonal(x).astype(F32)
        for core, row, col in diagonal_blocks(c):

            def subtract(scores, out):
                rows, cols = pl.ds(row, SHARD), pl.ds(col, 128)
                lse = col_lse[:, pl.ds(pl.multiple_of(core * PLANE + col, 128), 128)]
                out[rows, cols] = (weigh(scores[rows, cols], row_col[rows, :], lse) - mask).astype(BF16)

            @pl.when(c == core)
            def _():
                subtract(scores_own, own_out)

            @pl.when(c != core)
            def _():
                subtract(scores_other, other_out)

    row_sum = 0.5 * jnp.sum(row_lse[...], axis=1, keepdims=True)
    p_out[...] = jnp.broadcast_to(row_sum, (1, 128))
    col_sum = 0.5 * jnp.sum(col_lse[:, :COLS], axis=1, keepdims=True)
    q_out[...] = jnp.broadcast_to(col_sum, (1, 128)) - col_lse[:, COLS:]


def image_kernel(steps, at, own, other, txt_own, txt_other, q, *refs):
    z, first_core = at[2], at[3] == 0
    far = refs[0] if steps[0][2] is None else None
    outs, (rows_own, rows_other, total) = refs[0 if far is None else 1 : -3], refs[-3:]
    for i, (dz, _, _) in enumerate(steps):
        rows = pl.ds(pl.multiple_of(lax.rem(z + dz + NZ, NZ) * SHARD, SHARD), SHARD)
        rows_own[i * SHARD : (i + 1) * SHARD, :] = own[rows, :]
        rows_other[i * SHARD : (i + 1) * SHARD, :] = other[rows, :]
    chunk = 640

    @pl.loop(0, total.shape[1] // chunk)
    def _(i):
        cols = pl.ds(pl.multiple_of(i * chunk, chunk), chunk)
        total[:, cols] = jnp.dot(rows_own[...], txt_own[:, cols], preferred_element_type=F32) + jnp.dot(
            rows_other[...], txt_other[:, cols], preferred_element_type=F32
        )

    strips = total.shape[1] // 128
    for i, (_, out, place) in enumerate(steps):
        for j in range(strips):
            block = total[i * SHARD : (i + 1) * SHARD, columns(j)]
            if place is None:
                if out:
                    far_rows = far[part_of(far, 0, j, strips), :].astype(F32)
                    block += jnp.where(first_core == (out == 1), far_rows, 0.0)
                outs[out][:, columns(j)] = block
            else:
                outs[out][part_of(outs[out], place, j, strips), :] = block.astype(BF16)
    for ref in outs:
        if ref.shape[1] == 128:
            write_note(ref, q[...])


def text_kernel(at, own, received, img, img_other, p_own, p_other, *refs):
    sent, kept, p_out, total = refs[:3], refs[3], refs[4], refs[5]
    x, y, _, c = at
    p = p_own[...] + p_other[...]
    p_out[...] = p
    chunk = 512

    @pl.loop(0, PLANE // chunk)
    def _(i):
        cols = pl.ds(pl.multiple_of(i * chunk, chunk), chunk)
        total[cols, :] = lax.dot_general(
            own[:, cols], img[...], (((0,), (0,)), ((), ())), preferred_element_type=F32
        ) + lax.dot_general(
            received[:, cols], img_other[...], (((0,), (0,)), ((), ())), preferred_element_type=F32
        )

    strips = total.shape[1] // 128
    for d in range(4):
        for e in range(4):
            dx, dy = jnp.where(c == 0, e, d), jnp.where(c == 0, d, e)
            rows = pl.ds(block_row(x + dx, y + dy), SHARD)
            for i in range(strips):
                part = total[rows, columns(i)]
                if d == 0:
                    kept[e * SHARD : (e + 1) * SHARD, columns(i)] = part
                else:
                    sent[d - 1][part_of(sent[d - 1], e, i, strips), :] = part.astype(BF16)
        if d:
            write_note(sent[d - 1], p)


def image_middle_kernel(at, up, down, far, here, up_two, down_two, q, up_out, down_out, here_out, q_out):
    first_core = at[3] == 0
    strips = here.shape[1] // 128
    for i in range(strips):
        near, rest, cols = part_of(up, 0, i, strips), part_of(up, 1, i, strips), columns(i)
        here_out[:, cols] = here[:, cols] + up[near, :].astype(F32) + down[near, :].astype(F32)
        above = up_two[:, cols] + up[rest, :].astype(F32)
        below = down_two[:, cols] + down[rest, :].astype(F32)
        up_out[near, :] = above.astype(BF16)
        down_out[near, :] = below.astype(BF16)
    note_up, note_down, note_far = read_note(up), read_note(down), read_note(far)
    write_note(up_out, q[...] + note_up + jnp.where(first_core, note_far, 0.0))
    write_note(down_out, q[...] + note_down + jnp.where(first_core, 0.0, note_far))
    q_out[...] = q[...] + note_up + note_down


def text_middle_kernel(at, first, second, third, kept, p, *refs):
    sent, kept_out, p_out = refs[:3], refs[3], refs[4]
    total = p[...] + read_note(first) + read_note(second) + read_note(third)
    p_out[...] = total
    strips = kept.shape[1] // 128
    for e in range(4):
        for i in range(strips):
            rows, cols = part_of(first, e, i, strips), columns(i)
            part = kept[e * SHARD : (e + 1) * SHARD, cols] + first[rows, :].astype(F32)
            part += second[rows, :].astype(F32) + third[rows, :].astype(F32)
            if e == 0:
                kept_out[:, cols] = part
            else:
                sent[e - 1][part_of(first, 0, i, strips), :] = part.astype(BF16)
        if e:
            write_note(sent[e - 1], total)


def image_last_kernel(at, up, down, here, q, image_out, q_out):
    strips = here.shape[1] // 128
    for i in range(strips):
        rows, cols = part_of(up, 0, i, strips), columns(i)
        image = here[:, cols] + up[rows, :].astype(F32) + down[rows, :].astype(F32)
        image_out[:, cols] = image.astype(BF16)
    q_out[...] = q[...] + read_note(up) + read_note(down)


def text_last_kernel(at, first, second, third, kept, p, q, text_out, loss_out):
    strips = kept.shape[1] // 128
    for i in range(strips):
        rows, cols = part_of(first, 0, i, strips), columns(i)
        text = kept[:, cols] + first[rows, :].astype(F32) + second[rows, :].astype(F32) + third[rows, :].astype(F32)
        text_out[:, cols] = text.astype(BF16)
    loss = q[...] + p[...] + read_note(first) + read_note(second) + read_note(third)
    loss_out[...] = loss / (ROWS * NC * NX * NY)


def shards(image, text):
    embed = image.shape[1]
    scale = 4.0 / math.sqrt(embed)
    up, down = shift_z(image, 1), shift_z(image, -1)
    near = [shift_plane(text, d, True) for d in STEPS[1:]]
    line = pl.pallas_call(
        line_kernel,
        out_shape=jax.ShapeDtypeStruct((4 * SHARD, embed), BF16),
        in_specs=[pl.BlockSpec(memory_space=pltpu.HBM)] + [pl.BlockSpec(memory_space=pltpu.VMEM)] * 3,
        out_specs=pl.BlockSpec(memory_space=pltpu.VMEM),
        scratch_shapes=[pltpu.SemaphoreType.DMA],
        cost_estimate=pl.CostEstimate(flops=0, transcendentals=0, bytes_accessed=1 << 20),
        compiler_params=pltpu.CompilerParams(vmem_limit_bytes=4 << 20),
    )(text, *near)
    image_in = [image, up, down]
    up, down, line = lax.optimization_barrier((shift_z(up, 1), shift_z(down, -1), line))
    image_in += [up, down]
    far = [shift_plane(line, d, False) for d in STEPS[1:]]
    up, down = lax.optimization_barrier((shift_z(up, 1), shift_z(down, -1)))
    image_in += [up, down]
    line_sent, up = lax.optimization_barrier((line, up))
    last, *far = lax.optimization_barrier((shift_z(up, 1), *far))
    image_in.append(last)
    text_in = [line, *far]
    text_swapped = [swap_core(part) for part in (line_sent, *far)]

    tile = 2 * ROWS * COLS * embed
    half_scores_out = ((ROWS, PLANE), F32)
    lanes = ((ROWS, 128), F32)
    img, txt_own, scores_own, cols_own, top_own, sum_own = call(
        functools.partial(own_scores_kernel, scale),
        [((ROWS, embed), BF16), ((PLANE, embed), BF16), half_scores_out, ((1, PLANE), F32), lanes, lanes],
        image_in + text_in,
        [],
        tile // 2,
        ROWS * COLS,
        7 << 20,
        12,
    )
    txt_other, scores_other, row_lse, col_lse = call(
        functools.partial(other_scores_kernel, scale),
        [((PLANE, embed), BF16), half_scores_out, ((1, ROWS), F32), ((1, COLS + 128), F32)],
        [*text_swapped, img, scores_own, cols_own, top_own, sum_own],
        [pltpu.VMEM((1, PLANE), F32), pltpu.VMEM((ROWS, 128), F32), pltpu.VMEM((ROWS, 128), F32)],
        tile // 2,
        ROWS * COLS,
        7 << 20,
        14,
    )
    img_other = swap_core(img)
    col_lse = merge_columns(col_lse, swap_core(col_lse))
    for axis in (1, 0):
        col_lse = merge_columns(col_lse, *[shift_one(col_lse, axis, by) for by in STEPS[1:]])
    for bit in (1, 2, 4):
        row_lse = merge(row_lse, swap(row_lse, 2, bit))

    half = ((ROWS, PLANE), BF16)
    scalar = ((1, 128), F32)
    own, other, p, q = call(
        weights_kernel,
        [half, half, scalar, scalar],
        (scores_own, scores_other, row_lse, col_lse),
        [pltpu.VMEM((ROWS, 128), F32)],
        8 * ROWS * COLS,
        2 * ROWS * COLS,
        6 << 20,
        12,
    )
    received = swap_core(other)
    p_other = swap_core(p)
    message = lambda rows: ((rows * embed // 128 + NOTE, 128), BF16)
    image_part = lambda steps, outs, other, *far: call(
        functools.partial(image_kernel, steps),
        outs,
        (own, other, txt_own, txt_other, q, *far),
        [pltpu.VMEM((len(steps) * SHARD, PLANE), BF16)] * 2 + [pltpu.VMEM((len(steps) * SHARD, embed), F32)],
        tile // 2,
        0,
        8 << 20,
        16,
    )
    up, down, far = image_part(
        ((1, 0, 0), (3, 0, 1), (-1, 1, 0), (-3, 1, 1), (4, 2, 0)), [message(2 * SHARD)] * 2 + [message(SHARD)], other
    )
    received, up = lax.optimization_barrier((received, up))
    far = shift_far(far)
    *sent, kept, p = call(
        text_kernel,
        [message(4 * SHARD)] * 3 + [((4 * SHARD, embed), F32), scalar],
        (own, received, img, img_other, p, p_other),
        [pltpu.VMEM((PLANE, embed), F32)],
        tile // 2,
        0,
        12 << 20,
        24,
    )
    other, kept = lax.optimization_barrier((other, kept))
    here, up_two, down_two = image_part(
        ((0, 0, None), (2, 1, None), (-2, 2, None)), [((SHARD, embed), F32)] * 3, other, far
    )
    up, down, here = lax.optimization_barrier((up, down, here))
    up, down = shift_z(up, 1), shift_z(down, -1)
    sent = [shift_plane(part, d, True) for d, part in enumerate(sent, 1)]
    up, down, here, q = call(
        image_middle_kernel,
        [message(SHARD)] * 2 + [((SHARD, embed), F32), scalar],
        (up, down, far, here, up_two, down_two, q),
        [],
        1 << 20,
        0,
        2 << 20,
        12,
    )
    up, down = shift_z(up, 2), shift_z(down, -2)
    *sent, kept, p = call(
        text_middle_kernel,
        [message(SHARD)] * 3 + [((SHARD, embed), F32), scalar],
        (*sent, kept, p),
        [],
        1 << 20,
        0,
        4 << 20,
        12,
    )
    sent = [shift_plane(part, d, False) for d, part in enumerate(sent, 1)]
    image_grad, q = call(
        image_last_kernel,
        [((SHARD, embed), BF16), scalar],
        (up, down, here, q),
        [],
        1 << 19,
        0,
        1 << 20,
        8,
    )
    text_grad, loss = call(
        text_last_kernel,
        [((SHARD, embed), BF16), scalar],
        (*sent, kept, p, q),
        [],
        1 << 19,
        0,
        1 << 20,
        8,
    )
    return image_grad, text_grad, loss[0, 0]


def solution(mesh):
    return jax.shard_map(
        shards,
        mesh=mesh,
        in_specs=(P(("img", "txt"), None), P(("txt", "img"), None)),
        out_specs=(P(("img", "txt"), None), P(("txt", "img"), None), P()),
        check_vma=False,
    )
```

```python
import functools
import math

import jax
import jax.numpy as jnp
from jax import lax
from jax.experimental import pallas as pl
from jax.experimental.pallas import tpu as pltpu
from jax.sharding import PartitionSpec as P

NX, NY, NZ, NC = 4, 4, 8, 2
AXES = ("img", "txt")
SHARD = 64
HALF = SHARD // 2
ROWS = NZ * SHARD
PLANE = NX * NY * SHARD
COLS = NC * PLANE
NOTE = 16
BF16, F32 = jnp.bfloat16, jnp.float32


def device_id(x, y, z, c):
    return (((x % NX) * NY + y % NY) * NZ + z % NZ) * NC + c % NC


COORDINATES = [(x, y, z, c) for x in range(NX) for y in range(NY) for z in range(NZ) for c in range(NC)]


def shift_z(value, by):
    pairs = [(device_id(x, y, z, c), device_id(x, y, z + by, c)) for x, y, z, c in COORDINATES]
    return lax.ppermute(value, AXES, pairs)


def shift_plane(value, by, first):
    pairs = []
    for x, y, z, c in COORDINATES:
        along_y = (c == 0) == first
        to = (x, y + by) if along_y else (x + by, y)
        pairs.append((device_id(x, y, z, c), device_id(*to, z, c)))
    return lax.ppermute(value, AXES, pairs)


def shift_far(value):
    pairs = [(device_id(x, y, z, c), device_id(x, y, z + 2 - 4 * c, c)) for x, y, z, c in COORDINATES]
    return lax.ppermute(value, AXES, pairs)


def swap(value, axis, bit):
    pairs = []
    for at in COORDINATES:
        to = list(at)
        to[axis] ^= bit
        pairs.append((device_id(*at), device_id(*to)))
    return lax.ppermute(value, AXES, pairs)


def swap_core(value):
    return swap(value, 3, 1)


def merge(*parts):
    top = functools.reduce(jnp.maximum, parts)
    return top + jnp.log(sum(jnp.exp(part - top) for part in parts))


def merge_columns(*parts):
    lanes = lax.broadcasted_iota(jnp.int32, parts[0].shape, 1)
    return jnp.where(lanes < COLS, merge(*parts), sum(parts))


def shift_one(value, axis, by):
    pairs = []
    for at in COORDINATES:
        to = list(at)
        to[axis] += by
        pairs.append((device_id(*at), device_id(*to)))
    return lax.ppermute(value, AXES, pairs)


def position():
    img, txt = lax.axis_index("img"), lax.axis_index("txt")
    y = lax.rem(img, 2) * 2 + txt // (NZ * NC)
    return img // 2, y, lax.rem(txt // NC, NZ), lax.rem(txt, NC)


def call(kernel, outs, args, scratch, flops, transcendentals, moved, vmem_mib):
    vmem = pl.BlockSpec(memory_space=pltpu.VMEM)
    return pl.pallas_call(
        lambda *refs: kernel(position(), *refs),
        out_shape=[jax.ShapeDtypeStruct(shape, dtype) for shape, dtype in outs],
        in_specs=[vmem] * len(args),
        out_specs=[vmem] * len(outs),
        scratch_shapes=scratch,
        cost_estimate=pl.CostEstimate(flops=8 * flops, transcendentals=transcendentals, bytes_accessed=moved),
        compiler_params=pltpu.CompilerParams(vmem_limit_bytes=vmem_mib << 20),
    )(*args)


def diagonal_blocks(c):
    for zz in range(NZ):
        yield zz // 4, zz * SHARD, pl.multiple_of((zz % 4) * NY * SHARD + c * 2 * SHARD, 128)


def on_diagonal(x):
    rows = lax.broadcasted_iota(jnp.int32, (SHARD, 128), 0)
    lanes = lax.broadcasted_iota(jnp.int32, (SHARD, 128), 1)
    return lanes == rows + (x // 2) * SHARD


def has_diagonal(x, y, z):
    return z == (x % 2) * 4 + y


def block_row(xx, yy):
    return pl.multiple_of((lax.rem(xx + NX, NX) * NY + lax.rem(yy + NY, NY)) * SHARD, SHARD)


def write_note(ref, value):
    high = value.astype(BF16).astype(F32)
    middle = (value - high).astype(BF16).astype(F32)
    low = value - high - middle
    which = lax.broadcasted_iota(jnp.int32, (NOTE, 128), 0)
    rows = jnp.where(which == 0, high, jnp.where(which == 1, middle, jnp.where(which == 2, low, 0.0)))
    ref[ref.shape[0] - NOTE :, :] = rows.astype(BF16)


def read_note(ref):
    terms = [ref[ref.shape[0] - NOTE + i : ref.shape[0] - NOTE + i + 1, :].astype(F32) for i in range(3)]
    return terms[0] + terms[1] + terms[2]


def part_of(ref, index, strip, strips):
    start = (index * strips + strip) * SHARD
    return slice(start, start + SHARD)


def columns(strip):
    return slice(strip * 128, (strip + 1) * 128)


STEPS = (0, 1, -1, 2)


def place_text(at, core, parts, txt):
    x, y = at[0], at[1]
    for i, d in enumerate(STEPS):
        for j, e in enumerate(STEPS):
            dx, dy = jnp.where(core == 0, d, e), jnp.where(core == 0, e, d)
            txt[pl.ds(block_row(x - dx, y - dy), SHARD), :] = parts[i][j * SHARD : (j + 1) * SHARD, :]


def half_scores(scale, img, txt, scores, cols_out, row_top, row_sum):
    chunk = 512
    row_top[...] = jnp.full((ROWS, 128), -jnp.inf, F32)
    row_sum[...] = jnp.zeros((ROWS, 128), F32)

    def multiply(i):
        cols = slice(i * chunk, (i + 1) * chunk)
        scores[:, cols] = scale * lax.dot_general(
            img[...], txt[cols, :], (((1,), (1,)), ((), ())), preferred_element_type=F32
        )

    def reduce(i):
        cols = slice(i * chunk, (i + 1) * chunk)
        s = scores[:, cols]
        lanes = [s[:, j * 128 : (j + 1) * 128] for j in range(chunk // 128)]
        before = row_top[...]
        tops = functools.reduce(jnp.maximum, lanes, before)
        row_top[...] = tops
        row_sum[...] = row_sum[...] * jnp.exp(before - tops) + sum(jnp.exp(part - tops) for part in lanes)
        top = jnp.max(s, axis=0, keepdims=True)
        cols_out[:, cols] = top + jnp.log(jnp.sum(jnp.exp(s - top), axis=0, keepdims=True))

    multiply(0)
    for i in range(1, PLANE // chunk):
        reduce(i - 1)
        multiply(i)
    reduce(PLANE // chunk - 1)


def own_scores_kernel(scale, at, *refs):
    image_in, text_in = refs[:8], refs[8:12]
    img, txt, scores, cols_out, row_top, row_sum = refs[12:]
    for ref, step in zip(image_in, (0, -1, 1, -2, 2, -3, 3, -4)):
        where = lax.rem(at[2] + step + NZ, NZ) * SHARD
        img[pl.ds(pl.multiple_of(where, SHARD), SHARD), :] = ref[...]
    place_text(at, at[3], text_in, txt)
    half_scores(scale, img, txt, scores, cols_out, row_top, row_sum)


def other_scores_kernel(scale, at, *refs):
    text_in, (img, scores_own, cols_own, top_own, sum_own) = refs[:4], refs[4:9]
    txt, scores, row_out, col_out, cols_other, row_top, row_sum = refs[9:]
    x, y, z, c = at
    place_text(at, 1 - c, text_in, txt)
    half_scores(scale, img, txt, scores, cols_other, row_top, row_sum)
    top = jnp.max(jnp.maximum(row_top[...], top_own[...]), axis=1, keepdims=True)
    total = row_sum[...] * jnp.exp(row_top[...] - top) + sum_own[...] * jnp.exp(top_own[...] - top)
    row = top + jnp.log(jnp.sum(total, axis=1, keepdims=True))
    row_out[...] = jnp.transpose(jnp.broadcast_to(row, (ROWS, 128)))[0:1, :]
    col_out[:, pl.ds(pl.multiple_of(c * PLANE, PLANE), PLANE)] = cols_own[...]
    col_out[:, pl.ds(pl.multiple_of((1 - c) * PLANE, PLANE), PLANE)] = cols_other[...]
    col_out[:, COLS:] = jnp.zeros((1, 128), F32)

    @pl.when(has_diagonal(x, y, z))
    def _():
        mask = on_diagonal(x)
        total = jnp.zeros((1, 128), F32)
        for core, row, col in diagonal_blocks(c):
            rows, cols = slice(row, row + SHARD), pl.ds(col, 128)
            block = jnp.where(c == core, scores_own[rows, cols], scores[rows, cols])
            total += jnp.sum(jnp.where(mask, block, 0.0), axis=0, keepdims=True)
        col_out[:, COLS:] = jnp.broadcast_to(jnp.sum(total, axis=1, keepdims=True), (1, 128))


def line_kernel(text, *refs):
    near, line, sem = refs[:3], refs[3], refs[4]
    copy = pltpu.make_async_copy(text, line.at[pl.ds(0, SHARD)], sem)
    copy.start()
    for i, ref in enumerate(near, 1):
        line[i * SHARD : (i + 1) * SHARD, :] = ref[...]
    copy.wait()


def weights_kernel(at, scores_own, scores_other, row_lse, col_lse, own_out, other_out, p_out, q_out, row_col):
    x, y, z, c = at
    row_col[...] = jnp.transpose(jnp.broadcast_to(row_lse[...], (128, ROWS)))

    def weigh(s, rows, cols):
        return 0.5 * (jnp.exp(s - rows) + jnp.exp(s - cols))

    chunk = 256
    for half, scores, out in ((1 - c, scores_other, other_out), (c, scores_own, own_out)):

        @pl.loop(0, PLANE // chunk)
        def _(i, half=half, scores=scores, out=out):
            cols = pl.ds(pl.multiple_of(i * chunk, chunk), chunk)
            lse = col_lse[:, pl.ds(pl.multiple_of(half * PLANE + i * chunk, chunk), chunk)]
            rows = jnp.concatenate([row_col[...]] * (chunk // 128), axis=1)
            out[:, cols] = weigh(scores[:, cols], rows, lse).astype(BF16)

    @pl.when(has_diagonal(x, y, z))
    def _():
        mask = on_diagonal(x).astype(F32)
        for core, row, col in diagonal_blocks(c):

            def subtract(scores, out):
                rows, cols = pl.ds(row, SHARD), pl.ds(col, 128)
                lse = col_lse[:, pl.ds(pl.multiple_of(core * PLANE + col, 128), 128)]
                out[rows, cols] = (weigh(scores[rows, cols], row_col[rows, :], lse) - mask).astype(BF16)

            @pl.when(c == core)
            def _():
                subtract(scores_own, own_out)

            @pl.when(c != core)
            def _():
                subtract(scores_other, other_out)

    row_sum = 0.5 * jnp.sum(row_lse[...], axis=1, keepdims=True)
    p_out[...] = jnp.broadcast_to(row_sum, (1, 128))
    col_sum = 0.5 * jnp.sum(col_lse[:, :COLS], axis=1, keepdims=True)
    q_out[...] = jnp.broadcast_to(col_sum, (1, 128)) - col_lse[:, COLS:]


def image_kernel(steps, at, own, other, txt_own, txt_other, q, *refs):
    z, first_core = at[2], at[3] == 0
    far = refs[0] if steps[0][2] is None else None
    outs, (rows_own, rows_other, total) = refs[0 if far is None else 1 : -3], refs[-3:]
    for i, (dz, _, _) in enumerate(steps):
        rows = pl.ds(pl.multiple_of(lax.rem(z + dz + NZ, NZ) * SHARD, SHARD), SHARD)
        rows_own[i * SHARD : (i + 1) * SHARD, :] = own[rows, :]
        rows_other[i * SHARD : (i + 1) * SHARD, :] = other[rows, :]
    chunk = 1280

    @pl.loop(0, total.shape[1] // chunk)
    def _(i):
        cols = pl.ds(pl.multiple_of(i * chunk, chunk), chunk)
        total[:, cols] = jnp.dot(rows_own[...], txt_own[:, cols], preferred_element_type=F32) + jnp.dot(
            rows_other[...], txt_other[:, cols], preferred_element_type=F32
        )

    strips = total.shape[1] // 128
    for i, (_, out, place) in enumerate(steps):
        for j in range(strips):
            block = total[i * SHARD : (i + 1) * SHARD, columns(j)]
            if place is None:
                if out:
                    far_rows = far[part_of(far, 0, j, strips), :].astype(F32)
                    block += jnp.where(first_core == (out == 1), far_rows, 0.0)
                outs[out][:, columns(j)] = block
            else:
                outs[out][part_of(outs[out], place, j, strips), :] = block.astype(BF16)
    for ref in outs:
        if ref.shape[1] == 128:
            write_note(ref, q[...])


def text_kernel(at, own, received, img, img_other, p_own, p_other, *refs):
    sent, kept, p_out, total = refs[:3], refs[3], refs[4], refs[5]
    x, y, _, c = at
    p = p_own[...] + p_other[...]
    p_out[...] = p
    chunk = 512

    @pl.loop(0, PLANE // chunk)
    def _(i):
        cols = pl.ds(pl.multiple_of(i * chunk, chunk), chunk)
        total[cols, :] = lax.dot_general(
            own[:, cols], img[...], (((0,), (0,)), ((), ())), preferred_element_type=F32
        ) + lax.dot_general(
            received[:, cols], img_other[...], (((0,), (0,)), ((), ())), preferred_element_type=F32
        )

    strips = total.shape[1] // 128
    for d in range(4):
        for e in range(4):
            dx, dy = jnp.where(c == 0, e, d), jnp.where(c == 0, d, e)
            rows = pl.ds(block_row(x + dx, y + dy), SHARD)
            for i in range(strips):
                part = total[rows, columns(i)]
                if d == 0:
                    kept[e * SHARD : (e + 1) * SHARD, columns(i)] = part
                else:
                    sent[d - 1][part_of(sent[d - 1], e, i, strips), :] = part.astype(BF16)
        if d:
            write_note(sent[d - 1], p)


def image_middle_kernel(at, up, down, far, here, up_two, down_two, q, up_out, down_out, here_out, q_out):
    first_core = at[3] == 0
    strips = here.shape[1] // 128
    for i in range(strips):
        near, rest, cols = part_of(up, 0, i, strips), part_of(up, 1, i, strips), columns(i)
        here_out[:, cols] = here[:, cols] + up[near, :].astype(F32) + down[near, :].astype(F32)
        above = up_two[:, cols] + up[rest, :].astype(F32)
        below = down_two[:, cols] + down[rest, :].astype(F32)
        up_out[near, :] = above.astype(BF16)
        down_out[near, :] = below.astype(BF16)
    note_up, note_down, note_far = read_note(up), read_note(down), read_note(far)
    write_note(up_out, q[...] + note_up + jnp.where(first_core, note_far, 0.0))
    write_note(down_out, q[...] + note_down + jnp.where(first_core, 0.0, note_far))
    q_out[...] = q[...] + note_up + note_down


def text_middle_kernel(at, first, second, third, kept, p, *refs):
    sent, kept_out, p_out = refs[:3], refs[3], refs[4]
    total = p[...] + read_note(first) + read_note(second) + read_note(third)
    p_out[...] = total
    strips = kept.shape[1] // 128
    for e in range(4):
        for i in range(strips):
            rows, cols = part_of(first, e, i, strips), columns(i)
            part = kept[e * SHARD : (e + 1) * SHARD, cols] + first[rows, :].astype(F32)
            part += second[rows, :].astype(F32) + third[rows, :].astype(F32)
            if e == 0:
                kept_out[:, cols] = part
            else:
                sent[e - 1][part_of(first, 0, i, strips), :] = part.astype(BF16)
        if e:
            write_note(sent[e - 1], total)


def image_last_kernel(at, up, down, here, q, image_out, q_out):
    strips = here.shape[1] // 128
    for i in range(strips):
        rows, cols = part_of(up, 0, i, strips), columns(i)
        image = here[:, cols] + up[rows, :].astype(F32) + down[rows, :].astype(F32)
        image_out[:, cols] = image.astype(BF16)
    q_out[...] = q[...] + read_note(up) + read_note(down)


def text_last_kernel(at, first, second, third, kept, p, q, text_out, loss_out):
    strips = kept.shape[1] // 128
    for i in range(strips):
        rows, cols = part_of(first, 0, i, strips), columns(i)
        text = kept[:, cols] + first[rows, :].astype(F32) + second[rows, :].astype(F32) + third[rows, :].astype(F32)
        text_out[:, cols] = text.astype(BF16)
    loss = q[...] + p[...] + read_note(first) + read_note(second) + read_note(third)
    loss_out[...] = loss / (ROWS * NC * NX * NY)


def shards(image, text):
    embed = image.shape[1]
    scale = 4.0 / math.sqrt(embed)
    up, down = shift_z(image, 1), shift_z(image, -1)
    near = [shift_plane(text, d, True) for d in STEPS[1:]]
    line = pl.pallas_call(
        line_kernel,
        out_shape=jax.ShapeDtypeStruct((4 * SHARD, embed), BF16),
        in_specs=[pl.BlockSpec(memory_space=pltpu.HBM)] + [pl.BlockSpec(memory_space=pltpu.VMEM)] * 3,
        out_specs=pl.BlockSpec(memory_space=pltpu.VMEM),
        scratch_shapes=[pltpu.SemaphoreType.DMA],
        cost_estimate=pl.CostEstimate(flops=0, transcendentals=0, bytes_accessed=1 << 20),
        compiler_params=pltpu.CompilerParams(vmem_limit_bytes=4 << 20),
    )(text, *near)
    image_in = [image, up, down]
    up, down, line = lax.optimization_barrier((shift_z(up, 1), shift_z(down, -1), line))
    image_in += [up, down]
    far = [shift_plane(line, d, False) for d in STEPS[1:]]
    up, down = lax.optimization_barrier((shift_z(up, 1), shift_z(down, -1)))
    image_in += [up, down]
    line_sent, up = lax.optimization_barrier((line, up))
    last, *far = lax.optimization_barrier((shift_z(up, 1), *far))
    image_in.append(last)
    text_in = [line, *far]
    text_swapped = [swap_core(part) for part in (line_sent, *far)]

    tile = 2 * ROWS * COLS * embed
    half_scores_out = ((ROWS, PLANE), F32)
    lanes = ((ROWS, 128), F32)
    img, txt_own, scores_own, cols_own, top_own, sum_own = call(
        functools.partial(own_scores_kernel, scale),
        [((ROWS, embed), BF16), ((PLANE, embed), BF16), half_scores_out, ((1, PLANE), F32), lanes, lanes],
        image_in + text_in,
        [],
        tile // 2,
        ROWS * COLS,
        7 << 20,
        12,
    )
    txt_other, scores_other, row_lse, col_lse = call(
        functools.partial(other_scores_kernel, scale),
        [((PLANE, embed), BF16), half_scores_out, ((1, ROWS), F32), ((1, COLS + 128), F32)],
        [*text_swapped, img, scores_own, cols_own, top_own, sum_own],
        [pltpu.VMEM((1, PLANE), F32), pltpu.VMEM((ROWS, 128), F32), pltpu.VMEM((ROWS, 128), F32)],
        tile // 2,
        ROWS * COLS,
        7 << 20,
        14,
    )
    img_other = swap_core(img)
    col_lse = merge_columns(col_lse, swap_core(col_lse))
    for axis in (1, 0):
        col_lse = merge_columns(col_lse, *[shift_one(col_lse, axis, by) for by in STEPS[1:]])
    for bit in (1, 2, 4):
        row_lse = merge(row_lse, swap(row_lse, 2, bit))

    half = ((ROWS, PLANE), BF16)
    scalar = ((1, 128), F32)
    own, other, p, q = call(
        weights_kernel,
        [half, half, scalar, scalar],
        (scores_own, scores_other, row_lse, col_lse),
        [pltpu.VMEM((ROWS, 128), F32)],
        8 * ROWS * COLS,
        2 * ROWS * COLS,
        6 << 20,
        12,
    )
    received = swap_core(other)
    p_other = swap_core(p)
    message = lambda rows: ((rows * embed // 128 + NOTE, 128), BF16)
    image_part = lambda steps, outs, other, *far: call(
        functools.partial(image_kernel, steps),
        outs,
        (own, other, txt_own, txt_other, q, *far),
        [pltpu.VMEM((len(steps) * SHARD, PLANE), BF16)] * 2 + [pltpu.VMEM((len(steps) * SHARD, embed), F32)],
        tile // 2,
        0,
        8 << 20,
        16,
    )
    up, down, far = image_part(
        ((1, 0, 0), (3, 0, 1), (-1, 1, 0), (-3, 1, 1), (4, 2, 0)), [message(2 * SHARD)] * 2 + [message(SHARD)], other
    )
    received, up = lax.optimization_barrier((received, up))
    far = shift_far(far)
    *sent, kept, p = call(
        text_kernel,
        [message(4 * SHARD)] * 3 + [((4 * SHARD, embed), F32), scalar],
        (own, received, img, img_other, p, p_other),
        [pltpu.VMEM((PLANE, embed), F32)],
        tile // 2,
        0,
        12 << 20,
        24,
    )
    other, kept = lax.optimization_barrier((other, kept))
    here, up_two, down_two = image_part(
        ((0, 0, None), (2, 1, None), (-2, 2, None)), [((SHARD, embed), F32)] * 3, other, far
    )
    up, down, here = lax.optimization_barrier((up, down, here))
    up, down = shift_z(up, 1), shift_z(down, -1)
    sent = [shift_plane(part, d, True) for d, part in enumerate(sent, 1)]
    up, down, here, q = call(
        image_middle_kernel,
        [message(SHARD)] * 2 + [((SHARD, embed), F32), scalar],
        (up, down, far, here, up_two, down_two, q),
        [],
        1 << 20,
        0,
        2 << 20,
        12,
    )
    up, down = shift_z(up, 2), shift_z(down, -2)
    *sent, kept, p = call(
        text_middle_kernel,
        [message(SHARD)] * 3 + [((SHARD, embed), F32), scalar],
        (*sent, kept, p),
        [],
        1 << 20,
        0,
        4 << 20,
        12,
    )
    sent = [shift_plane(part, d, False) for d, part in enumerate(sent, 1)]
    image_grad, q = call(
        image_last_kernel,
        [((SHARD, embed), BF16), scalar],
        (up, down, here, q),
        [],
        1 << 19,
        0,
        1 << 20,
        8,
    )
    text_grad, loss = call(
        text_last_kernel,
        [((SHARD, embed), BF16), scalar],
        (*sent, kept, p, q),
        [],
        1 << 19,
        0,
        1 << 20,
        8,
    )
    return image_grad, text_grad, loss[0, 0]


def solution(mesh):
    return jax.shard_map(
        shards,
        mesh=mesh,
        in_specs=(P(("img", "txt"), None), P(("txt", "img"), None)),
        out_specs=(P(("img", "txt"), None), P(("txt", "img"), None), P()),
        check_vma=False,
    )
```
